256 devices in a mesh: grp: 16 (over y, x), sp: 16 (over z, core).
Axes of the slice: x: 4, y: 4, z: 8, core: 2. Of those that a mesh axis runs over, the one named last changes fastest.
Arguments:
- latents: bfloat16 [128, 512, 1152], P('grp', 'sp'), may hold values from -6 to 6
- route: int32 [128], replicated, may hold values from 0 to 127, as said below
- counts: int32 [16, 4], P('grp'), may hold values from 1 to 3, 8 in all within a row
- modulation: float32 [64, 3, 1152], P('grp'), may hold values from -4 to 4
- w_qkv: bfloat16 [1152, 3456], replicated, may hold values from -0.1875 to 0.1875
- w_out: bfloat16 [1152, 1152], replicated, may hold values from -0.1875 to 0.1875
- cotangent: bfloat16 [128, 512, 1152], P('grp', 'sp'), may hold values from -6 to 6
Outputs:
- output: bfloat16 [128, 512, 1152], P('grp', 'sp')
- grad_in: bfloat16 [128, 512, 1152], P('grp', 'sp')
The draws below stay inside these ranges and needn't reach their ends.
Inputs may be any that keep to these rules, and one draw needn't show every extreme that they name: `route`: a permutation; entry g * 8 + s is the balanced slot of frame s of group g, and the balanced slot's group is its value divided by 8; no group hands more than 2 frames to one group, and some pair of groups has exactly 2. `counts`: each group's clips fill its 8 balanced frames in order.
All inputs are finite; a program needn't handle non-finite values.
Results may differ from the reference program's by a relative error of at most 0.03.
Values may be sent and summed in bfloat16 or wider, within the bound.
A program may use at most 128 MiB of HBM per device.

```python
import math
import jax
import jax.numpy as jnp
import numpy as np
from jax import lax

D = 1152
HEAD_DIM = 72
F_GRP = 8
CLIPS = 4
CLIP_MOST = 3
CAP = 2
FRAME_TOK = 512
FRAMES = 128
NCLIPS = 64
N_GRP = 16


def draw_route(key, part):
    key = jax.random.fold_in(key, 7)
    subkeys = jax.random.split(key, 4)
    heavy = jax.random.randint(subkeys[0], (), 0, N_GRP)
    entries = N_GRP * CAP
    values = (jnp.arange(entries, dtype=jnp.int32) // CAP).astype(jnp.int32)
    copies = (jnp.arange(entries, dtype=jnp.int32) % CAP).astype(jnp.int32)
    needed = (values == 1) | (values == N_GRP - 1) | (values == N_GRP // 2)
    tier = jnp.where(values == heavy, 0, jnp.where(needed & (copies == 0), 1, 2)).astype(jnp.int32)
    ranks = jax.random.permutation(subkeys[1], entries).astype(jnp.int32)
    score = tier * entries + ranks
    chosen = jnp.argsort(score, stable=True)[:F_GRP]
    offsets = values[chosen].astype(jnp.int32)
    offsets = jax.random.permutation(subkeys[2], offsets)
    orders = jax.vmap(lambda subkey: jax.random.permutation(subkey, F_GRP))(jax.random.split(subkeys[3], N_GRP))
    sources = jnp.arange(N_GRP, dtype=jnp.int32)[:, None]
    target_group = (sources + offsets[None, :]) % N_GRP
    target_slot = orders[target_group, jnp.arange(F_GRP, dtype=jnp.int32)[None, :]]
    return (target_group * F_GRP + target_slot).reshape(-1).astype(jnp.int32)


def block_scale(own_key, dims, pieces, least, high):
    level = 1.0
    for position, blocks in pieces:
        steps = jax.random.uniform(jax.random.fold_in(jax.random.fold_in(own_key, 6), position), (blocks,), jnp.float32, least / len(pieces), high / len(pieces))
        level = level * jnp.repeat(jnp.exp(steps), dims[position] // blocks).reshape((-1,) + (1,) * (len(dims) - 1 - position))
    return level


def profile(number_of, total, limit, lean):
    portions = [(1 << 20) // math.isqrt(standing ** lean) + 1 for standing in range(2, number_of + 1)]
    surplus, holding = total - limit - (number_of - 1), [1] * (number_of - 1)
    while surplus > 0:
        candidates = [i for i in range(number_of - 1) if holding[i] < limit]
        pool, remaining = sum([portions[i] for i in candidates]), surplus
        for i in candidates:
            extra = min(limit - holding[i], max(1, remaining * portions[i] // pool), surplus)
            holding[i] = holding[i] + extra
            surplus = surplus - extra
    return np.array([limit] + holding)


def ragged(rng, amount, total, reach, lean):
    if amount == 2:
        one = jax.random.randint(rng, (), max(1, total - reach), min(reach, total - 1) + 1)
        return jnp.stack([one, total - one])
    lengths = jnp.asarray(profile(amount, total, reach, lean), jnp.int32)
    twos = (amount - 1) // 2
    donor, sink = lengths[1:1 + 2 * twos:2], lengths[2:2 + 2 * twos:2]
    margin = jnp.minimum(donor - 1, reach - sink)
    moved = jax.random.randint(jax.random.fold_in(rng, 1), (twos,), 0, 1 << 20) % (margin + 1)
    lengths = lengths.at[1:1 + 2 * twos:2].set(donor - moved).at[2:2 + 2 * twos:2].set(sink + moved)
    return lengths[jax.random.permutation(jax.random.fold_in(rng, 2), amount)]


def centred(stream_key, extent, scale, bound, pieces=(), held_as=jnp.bfloat16):
    values = jax.random.normal(stream_key, extent, jnp.float32) * scale
    if len(pieces) > 0:
        values = block_scale(stream_key, extent, pieces, -0.22, 0.18) * values
    return jnp.clip(values, min=-bound, max=bound).astype(held_as)


def setup_inputs(seed: int = 0) -> dict:
    key_of = jax.random.split(jax.random.key(seed), 8)
    latents = centred(key_of[0], (FRAMES, FRAME_TOK, D), 1.0, 6.0, ((0, 16), (1, 16)))
    route = draw_route(jax.random.fold_in(key_of[7], 71), 0)
    counts = jax.vmap(lambda own: ragged(own, CLIPS, F_GRP, CLIP_MOST, 1))(jax.random.split(key_of[2], N_GRP)).reshape((N_GRP, CLIPS)).astype(jnp.int32)
    modulation = centred(key_of[3], (NCLIPS, 3, D), 1.0, 4.0, ((0, 16),), jnp.float32)
    w_qkv = centred(key_of[4], (D, 3 * D), D ** -0.5, 0.1875)
    w_out = centred(key_of[5], (D, D), D ** -0.5, 0.1875)
    cotangent = centred(key_of[6], (FRAMES, FRAME_TOK, D), 1.0, 6.0, ((0, 16), (1, 16)))
    return {"latents": latents, "route": route, "counts": counts, "modulation": modulation, "w_qkv": w_qkv, "w_out": w_out, "cotangent": cotangent}


epsilon = 1e-06

def modulate_norm(x_float, shifts, scales):
    center = lax.optimization_barrier(jnp.mean(x_float, axis=-1, keepdims=True))
    spread = x_float - center
    variance = lax.optimization_barrier(jnp.mean(spread * spread, axis=-1, keepdims=True))
    return (spread * lax.rsqrt(variance + epsilon) * (1.0 + scales) + shifts).astype(jnp.bfloat16)

def attend(query, keys, values, head_dim):
    positions = query.shape[0]
    heads = query.shape[1] // head_dim
    q_float = query.reshape(positions, heads, head_dim).astype(jnp.float32)
    k_float = keys.reshape(positions, heads, head_dim).astype(jnp.float32)
    v_float = values.reshape(positions, heads, head_dim).astype(jnp.float32)
    scores = jnp.einsum('qhd,khd->hqk', q_float, k_float) * head_dim ** (-0.5)
    probs = jax.nn.softmax(scores, axis=-1).astype(jnp.bfloat16)
    mixed = jnp.einsum('hqk,khd->qhd', probs.astype(jnp.float32), v_float)
    return mixed.astype(jnp.bfloat16).reshape(query.shape)

def frame_out(frame, frame_mod, w_qkv, w_out):
    x_float = frame.astype(jnp.float32)
    normed = modulate_norm(x_float, frame_mod[0], frame_mod[1])
    qkv_rows = jnp.dot(normed, w_qkv, preferred_element_type=jnp.float32).astype(jnp.bfloat16)
    query, keys, values = jnp.split(qkv_rows, 3, axis=1)
    attended = attend(query, keys, values, HEAD_DIM)
    projected = jnp.dot(attended, w_out, preferred_element_type=jnp.float32)
    return (x_float + frame_mod[2] * projected).astype(jnp.bfloat16)

def reference(latents, route, counts, modulation, w_qkv, w_out, cotangent):
    placed = jnp.zeros_like(latents).at[route].set(latents)
    clip_ends = jnp.cumsum(counts, axis=1).astype(jnp.int32)
    slot_ids = jnp.arange(F_GRP, dtype=jnp.int32)
    clip_of = lax.optimization_barrier(jnp.sum((slot_ids[None, :, None] >= clip_ends[:, None, :]).astype(jnp.int32), axis=2))
    clip_index = (jnp.arange(N_GRP, dtype=jnp.int32)[:, None] * CLIPS + clip_of).reshape(-1).astype(jnp.int32)
    frame_mods = modulation[clip_index]

    def per_frame(frame_args):
        frame, frame_mod, grad_frame = frame_args
        result, puller = jax.vjp(lambda inner: frame_out(inner, frame_mod, w_qkv, w_out), frame)
        grad_frame_in, = puller(grad_frame)
        return (result, grad_frame_in)
    output, grad_balanced = lax.map(per_frame, (placed, frame_mods, cotangent))
    grad_in = grad_balanced[route]
    return (output, grad_in)
```

```python
import functools
import math

import jax
import jax.numpy as jnp
from jax import lax
from jax.experimental import pallas as pl
from jax.experimental.pallas import tpu as pltpu
from jax.sharding import PartitionSpec as P

MESH = pl.DeviceIdType.MESH
HEADS = 16
LANES = 128
EPS = 1e-06
NT = (((1,), (1,)), ((), ()))
NN = (((1,), (0,)), ((), ()))
TN = (((0,), (0,)), ((), ()))
BF = jnp.bfloat16
F32 = jnp.float32


def dot(a, b, dims):
    return lax.dot_general(a, b, dims, preferred_element_type=F32)


def offsets(groups, frames):
    ct_send = 0
    ct_recv = ct_send + 2 * groups
    out_send = ct_recv + frames
    out_recv = out_send + 2 * groups
    mod_send = out_recv + frames
    mod_recv = mod_send + groups
    return ct_send, ct_recv, out_send, out_recv, mod_send, mod_recv


def kernel(
    groups,
    tab,
    lat,
    ct,
    mod,
    wqkv_hbm,
    wout_hbm,
    out_ref,
    grad_ref,
    wqkv,
    wout,
    ct_send,
    ct_recv,
    ct_stage,
    ct_rows,
    out_stage,
    out_mid,
    out_send,
    out_recv,
    grad_stage,
    mod_send,
    mod_recv,
    modf,
    x_rows,
    normed,
    qkv,
    qp,
    kp,
    vp,
    probs,
    op,
    att,
    dop,
    dk_own,
    dv_own,
    part_send,
    part_recv,
    w_sem,
    loc_sem,
    xs,
    xr,
    ms,
    mr,
    cs,
    cr,
    czs,
    czr,
    kvs,
    kvr,
    ozs,
    ozr,
    os_,
    or_,
    ps,
    pr,
    gs,
    gr,
):
    frames, rows, width = ct.shape
    head = width // HEADS
    zs = frames
    half = frames * rows
    me = lax.axis_index("grp")
    sp = lax.axis_index("sp")
    z = sp // 2
    core = sp % 2
    o_cts, o_ctr, o_os, o_or, o_ms, o_mr = offsets(groups, frames)

    def z_dev(d):
        return {"sp": lax.rem(z + d, zs) * 2 + core}

    def g_dev(d):
        return {"grp": lax.rem(me + d, groups)}

    other = {"sp": z * 2 + (1 - core)}

    w1 = pltpu.make_async_copy(wqkv_hbm, wqkv, w_sem.at[0])
    w2 = pltpu.make_async_copy(wout_hbm, wout, w_sem.at[1])
    w1.start()
    w2.start()

    barrier = pltpu.get_barrier_semaphore()
    for d in range(1, zs):
        pl.semaphore_signal(barrier, inc=1, device_id=z_dev(d), device_id_type=MESH)
    for d in range(1, groups):
        pl.semaphore_signal(barrier, inc=1, device_id=g_dev(d), device_id_type=MESH)
    pl.semaphore_signal(barrier, inc=1, device_id=other, device_id_type=MESH)

    for g in range(groups):
        mod_send[g] = mod[tab[o_ms + g]]
    for i in range(2 * groups):
        ct_send[i // 2, i % 2] = ct[tab[o_cts + i]]

    pl.semaphore_wait(barrier, zs - 1 + groups - 1 + 1)

    def remote(src, dst, s_sem, r_sem, dev):
        return pltpu.make_async_remote_copy(
            src_ref=src, dst_ref=dst, send_sem=s_sem, recv_sem=r_sem, device_id=dev, device_id_type=MESH
        )

    def group_copies(src, dst, s_sem, r_sem):
        own = pltpu.make_async_copy(src.at[me], dst.at[me], s_sem.at[0])
        return [own] + [
            remote(src.at[lax.rem(me + d, groups)], dst.at[me], s_sem.at[d], r_sem.at[d], g_dev(d))
            for d in range(1, groups)
        ]

    def z_copies(src, dst, s_sem, r_sem):
        own = pltpu.make_async_copy(src.at[z], dst.at[z], s_sem.at[0])
        return [own] + [
            remote(src.at[lax.rem(z + d, zs)], dst.at[z], s_sem.at[d], r_sem.at[d], z_dev(d))
            for d in range(1, zs)
        ]

    def start(copies):
        for copy in copies:
            copy.start()

    def wait_recv(copies):
        copies[0].wait()
        for copy in copies[1:]:
            copy.wait_recv()

    def wait_send(copies):
        for copy in copies[1:]:
            copy.wait_send()

    mod_c = group_copies(mod_send, mod_recv, ms, mr)
    x_c = z_copies(lat, x_rows, xs, xr)
    ct_c = group_copies(ct_send, ct_recv, cs, cr)
    start(mod_c)
    start(x_c)
    start(ct_c)

    qkv[:, 3 * width :] = jnp.zeros((half, qkv.shape[1] - 3 * width), BF)
    wait_recv(mod_c)
    mine = mod_recv[tab[o_mr]]
    tiles = width // LANES
    for i in range(3):
        for t in range(tiles):
            modf[i : i + 1, t * LANES : (t + 1) * LANES] = mine[i * tiles + t : i * tiles + t + 1, :]
    wait_recv(x_c)

    def norm_parts(r):
        x = x_rows[r].astype(F32)
        center = jnp.mean(x, axis=-1, keepdims=True)
        spread = x - center
        inv = lax.rsqrt(jnp.mean(spread * spread, axis=-1, keepdims=True) + EPS)
        return x, spread * inv, inv

    def norm_step(r, carry):
        _, xhat, _ = norm_parts(r)
        normed[pl.ds(r * rows, rows), :] = (xhat * (1.0 + modf[1:2, :]) + modf[0:1, :]).astype(BF)
        return carry

    lax.fori_loop(0, frames, norm_step, 0)

    w1.wait()
    lane = lax.broadcasted_iota(jnp.int32, (half, LANES), 1)

    def project(start_col, tile, count):
        def step(i, carry):
            cols = pl.ds(pl.multiple_of(start_col + i * tile, LANES), tile)
            qkv[:, cols] = dot(normed[...], wqkv[:, cols], NN).astype(BF)
            return carry

        lax.fori_loop(0, count, step, 0)

    def padded(source, start_col):
        piece = source[:, start_col : start_col + LANES]
        return jnp.where(lane < head, piece, jnp.zeros_like(piece))

    project(width, 256, 2 * width // 256)
    for h in range(HEADS):
        spot = slice(h * LANES, (h + 1) * LANES)
        kp[0, :, spot] = padded(qkv, width + h * head)
        vp[0, :, spot] = padded(qkv, 2 * width + h * head)
    k_c = remote(kp.at[0], kp.at[1], kvs.at[0], kvr.at[0], other)
    v_c = remote(vp.at[0], vp.at[1], kvs.at[1], kvr.at[1], other)
    k_c.start()
    v_c.start()
    project(0, 384, width // 384)
    for h in range(HEADS):
        qp[:, h * LANES : (h + 1) * LANES] = padded(qkv, h * head)
    k_c.wait_recv()
    v_c.wait_recv()

    factor = head**-0.5
    log2 = factor * math.log2(math.e)
    unroll = 2

    def spot_of(h):
        return pl.ds(pl.multiple_of(h * LANES, LANES), LANES)

    def forward_step(i, carry):
        for u in range(unroll):
            h = i * unroll + u
            spot = spot_of(h)
            k = kp[:, :, spot].reshape(2 * half, LANES)
            v = vp[:, :, spot].reshape(2 * half, LANES)
            scores = dot(k, qp[:, spot], NT)
            top = jnp.max(scores, axis=0, keepdims=True)
            ex = jnp.exp2((scores - top) * log2)
            p = (ex * (1.0 / jnp.sum(ex, axis=0, keepdims=True))).astype(BF)
            probs[h] = p
            op[:, spot] = dot(v, p, TN).T.astype(BF)
        return carry

    lax.fori_loop(0, HEADS // unroll, forward_step, 0)
    for h in range(HEADS):
        att[:, h * head : (h + 1) * head] = op[:, h * LANES : h * LANES + head]

    w2.wait()

    def out_step(i, carry):
        cols = pl.ds(pl.multiple_of(i * 384, LANES), 384)
        proj = dot(att[...], wout[:, cols], NN)
        x = x_rows[:, :, cols].reshape(half, 384).astype(F32)
        out_stage[:, :, cols] = (x + modf[2:3, cols] * proj).astype(BF).reshape(frames, rows, 384)
        return carry

    lax.fori_loop(0, width // 384, out_step, 0)
    oz_c = z_copies(out_stage, out_mid, ozs, ozr)
    start(oz_c)

    wait_recv(ct_c)
    for f in range(frames):
        slot = tab[o_ctr + f]
        ct_stage[f] = ct_recv[slot // 2, slot % 2]
    cz_c = z_copies(ct_stage, ct_rows, czs, czr)
    start(cz_c)

    wait_recv(oz_c)
    for i in range(2 * groups):
        out_send[i // 2, i % 2] = out_mid[tab[o_os + i]]
    o_c = group_copies(out_send, out_recv, os_, or_)
    start(o_c)

    wait_recv(cz_c)

    def gated_step(r, carry):
        normed_rows = pl.ds(r * rows, rows)
        att[normed_rows, :] = (ct_rows[r].astype(F32) * modf[2:3, :]).astype(BF)
        return carry

    lax.fori_loop(0, frames, gated_step, 0)

    def back_out_step(i, carry):
        cols = pl.ds(pl.multiple_of(i * 384, LANES), 384)
        qkv[:, cols] = dot(att[...], wout[cols, :], NT).astype(BF)
        return carry

    lax.fori_loop(0, width // 384, back_out_step, 0)
    for h in range(HEADS):
        dop[:, h * LANES : (h + 1) * LANES] = padded(qkv, h * head)

    segments = part_send.shape[0]
    per = HEADS // segments

    def backward_step(seg, i, carry):
        for u in range(unroll):
            j = i * unroll + u
            h = seg * per + j
            spot = spot_of(h)
            k = kp[:, :, spot].reshape(2 * half, LANES)
            v = vp[:, :, spot].reshape(2 * half, LANES)
            do = dop[:, spot]
            p = probs[h]
            p_wide = p.astype(F32)
            weighted = p_wide * dot(v, do, NT)
            total = jnp.sum(weighted, axis=0, keepdims=True)
            ds = ((weighted - p_wide * total) * factor).astype(BF)
            dv = dot(p, do, NN)
            dk = dot(ds, qp[:, spot], NN)
            op[:, spot] = dot(k, ds, TN).T.astype(BF)
            dk_own[:, spot] = dk[:half]
            dv_own[:, spot] = dv[:half]
            part_send[seg, 0, :, spot_of(j)] = dk[half:].astype(BF)
            part_send[seg, 1, :, spot_of(j)] = dv[half:].astype(BF)
        return carry

    part_c = []
    for seg in range(segments):
        lax.fori_loop(0, per // unroll, functools.partial(backward_step, seg), 0)
        copy = remote(part_send.at[seg], part_recv.at[seg], ps.at[seg], pr.at[seg], other)
        copy.start()
        part_c.append(copy)
    for h in range(HEADS):
        qkv[:, h * head : (h + 1) * head] = op[:, h * LANES : h * LANES + head]
    for seg in range(segments):
        part_c[seg].wait_recv()
        for j in range(per):
            h = seg * per + j
            spot = slice(h * LANES, (h + 1) * LANES)
            there = slice(j * LANES, (j + 1) * LANES)
            dk = (dk_own[:, spot] + part_recv[seg, 0, :, there].astype(F32)).astype(BF)
            dv = (dv_own[:, spot] + part_recv[seg, 1, :, there].astype(F32)).astype(BF)
            qkv[:, width + h * head : width + (h + 1) * head] = dk[:, :head]
            qkv[:, 2 * width + h * head : 2 * width + (h + 1) * head] = dv[:, :head]

    def back_in_step(i, carry):
        cols = pl.ds(pl.multiple_of(i * 384, LANES), 384)
        att[:, cols] = dot(qkv[:, : 3 * width], wqkv[cols, :], NT).astype(BF)
        return carry

    lax.fori_loop(0, width // 384, back_in_step, 0)

    def grad_step(r, carry):
        _, xhat, inv = norm_parts(r)
        dhat = att[pl.ds(r * rows, rows), :].astype(F32) * (1.0 + modf[1:2, :])
        m1 = jnp.mean(dhat, axis=-1, keepdims=True)
        m2 = jnp.mean(dhat * xhat, axis=-1, keepdims=True)
        grad_stage[r] = (ct_rows[r].astype(F32) + inv * (dhat - m1 - xhat * m2)).astype(BF)
        return carry

    lax.fori_loop(0, frames, grad_step, 0)
    gz_c = z_copies(grad_stage, grad_ref, gs, gr)
    start(gz_c)

    wait_recv(o_c)
    for f in range(frames):
        slot = tab[o_or + f]
        out_ref[f] = out_recv[slot // 2, slot % 2]
    wait_recv(gz_c)

    for copies in (mod_c, x_c, ct_c, oz_c, cz_c, o_c, gz_c):
        wait_send(copies)
    k_c.wait_send()
    v_c.wait_send()
    for copy in part_c:
        copy.wait_send()


def tables(route, counts, groups, frames, me, z):
    target = route.reshape(groups, frames)
    to, slot = target // frames, target % frames
    ids = jnp.arange(frames, dtype=jnp.int32)
    same = to[:, :, None] == to[:, None, :]
    rank = jnp.sum((same & (ids[None, None, :] < ids[None, :, None])).astype(jnp.int32), axis=2)
    group_ids = jnp.arange(groups, dtype=jnp.int32)
    place = jnp.arange(2, dtype=jnp.int32)
    here = to == me
    my_to = lax.dynamic_index_in_dim(to, me, 0, False)
    my_rank = lax.dynamic_index_in_dim(rank, me, 0, False)
    ct_send = jnp.sum(
        jnp.where(here[:, None, :] & (rank[:, None, :] == place[None, :, None]), slot[:, None, :], 0), axis=2
    )
    ct_recv = my_to * 2 + my_rank
    out_send = jnp.sum(
        jnp.where(
            (my_to[None, None, :] == group_ids[:, None, None]) & (my_rank[None, None, :] == place[None, :, None]),
            ids[None, None, :],
            0,
        ),
        axis=2,
    )
    origin = group_ids[:, None] * 2 + rank
    out_recv = jnp.sum(jnp.where((here & (slot == ids[:, None, None])), origin[None], 0), axis=(1, 2))
    ends = jnp.cumsum(counts[0])
    clip_of = jnp.sum((ids[:, None] >= ends[None, :]).astype(jnp.int32), axis=1)
    z_to = lax.dynamic_index_in_dim(to, z, 1, False)
    z_slot = lax.dynamic_index_in_dim(slot, z, 1, False)
    mod_send = jnp.sum(
        jnp.where((z_slot[:, None] == ids[None, :]) & (z_to == me)[:, None], clip_of[None, :], 0), axis=1
    )
    mod_recv = lax.dynamic_index_in_dim(my_to, z, 0, True)
    parts = [ct_send.reshape(-1), ct_recv, out_send.reshape(-1), out_recv, mod_send, mod_recv]
    return jnp.concatenate(parts).astype(jnp.int32)


def local(latents, route, counts, modulation, w_qkv, w_out, cotangent):
    frames, rows, width = latents.shape
    groups = lax.axis_size("grp")
    me = lax.axis_index("grp")
    z = lax.axis_index("sp") // 2
    table = tables(route, counts, groups, frames, me, z)
    clips = modulation.shape[0]
    mod_rows = 3 * width // LANES
    mod_pad = -(-mod_rows // 8) * 8
    mod = jnp.pad(modulation.reshape(clips, mod_rows, LANES), ((0, 0), (0, mod_pad - mod_rows), (0, 0)))
    half = frames * rows
    padded = HEADS * LANES
    segments = 4
    piece = (frames, rows, width)
    slots = (groups, 2, rows, width)
    dma = pltpu.SemaphoreType.DMA
    vmem = pltpu.VMEM
    block = jax.ShapeDtypeStruct(piece, BF)
    scratch = [
        vmem(w_qkv.shape, BF),
        vmem(w_out.shape, BF),
        vmem(slots, BF),
        vmem(slots, BF),
        vmem(piece, BF),
        vmem(piece, BF),
        vmem(piece, BF),
        vmem(piece, BF),
        vmem(slots, BF),
        vmem(slots, BF),
        vmem(piece, BF),
        vmem((groups, mod_pad, LANES), F32),
        vmem((groups, mod_pad, LANES), F32),
        vmem((8, width), F32),
        vmem(piece, BF),
        vmem((half, width), BF),
        vmem((half, 3 * width + LANES), BF),
        vmem((half, padded), BF),
        vmem((2, half, padded), BF),
        vmem((2, half, padded), BF),
        vmem((HEADS, 2 * half, half), BF),
        vmem((half, padded), BF),
        vmem((half, width), BF),
        vmem((half, padded), BF),
        vmem((half, padded), F32),
        vmem((half, padded), F32),
        vmem((segments, 2, half, padded // segments), BF),
        vmem((segments, 2, half, padded // segments), BF),
        dma((2,)),
        dma((2,)),
        dma((frames,)),
        dma((frames,)),
        dma((groups,)),
        dma((groups,)),
        dma((groups,)),
        dma((groups,)),
        dma((frames,)),
        dma((frames,)),
        dma((2,)),
        dma((2,)),
        dma((frames,)),
        dma((frames,)),
        dma((groups,)),
        dma((groups,)),
        dma((segments,)),
        dma((segments,)),
        dma((frames,)),
        dma((frames,)),
    ]
    in_vmem = pl.BlockSpec(memory_space=vmem)
    anywhere = pl.BlockSpec(memory_space=pl.ANY)
    return pl.pallas_call(
        functools.partial(kernel, groups),
        out_shape=(block, block),
        in_specs=[pl.BlockSpec(memory_space=pltpu.SMEM), anywhere, in_vmem, in_vmem, anywhere, anywhere],
        out_specs=(in_vmem, in_vmem),
        scratch_shapes=scratch,
        compiler_params=pltpu.CompilerParams(
            collective_id=0, has_side_effects=True, vmem_limit_bytes=60 * 1024 * 1024
        ),
    )(table, latents, cotangent, mod, w_qkv, w_out)


def solution(mesh):
    rows = P("grp", "sp", None)
    return jax.shard_map(
        local,
        mesh=mesh,
        in_specs=(rows, P(), P("grp", None), P("grp", None, None), P(), P(), rows),
        out_specs=(rows, rows),
        check_vma=False,
    )
```

```python
import functools
import math

import jax
import jax.numpy as jnp
from jax import lax
from jax.experimental import pallas as pl
from jax.experimental.pallas import tpu as pltpu
from jax.sharding import PartitionSpec as P

MESH = pl.DeviceIdType.MESH
HEADS = 16
LANES = 128
EPS = 1e-06
NT = (((1,), (1,)), ((), ()))
NN = (((1,), (0,)), ((), ()))
TN = (((0,), (0,)), ((), ()))
BF = jnp.bfloat16
F32 = jnp.float32


def dot(a, b, dims):
    return lax.dot_general(a, b, dims, preferred_element_type=F32)


def bits_of(number):
    return number.bit_length() - 1


def colour(route_row, groups, frames):
    edges = groups * frames
    shift = bits_of(frames)
    square = (edges, edges)
    r_wide = jnp.broadcast_to(route_row.astype(F32), square)
    r_row, r_col = r_wide.astype(jnp.int32), r_wide.T.astype(jnp.int32)
    k_row = lax.broadcasted_iota(jnp.int32, square, 1)
    k_col = lax.broadcasted_iota(jnp.int32, square, 0)
    same_source = (k_row >> shift) == (k_col >> shift)
    same_target = (r_row >> shift) == (r_col >> shift)
    as_bf = lambda flag: jnp.where(flag, 1.0, 0.0).astype(BF)
    eye = jnp.where(k_row == k_col, 1.0, 0.0)
    c_row = jnp.zeros((1, edges), jnp.int32)
    c_col = jnp.zeros((edges, 1), jnp.int32)
    for level in range(shift):
        same = c_row == c_col
        s_pair = as_bf(same & same_source & ((k_row >> level) == ((k_col >> level) ^ 1)))
        t_pair = as_bf(same & same_target & ((r_row >> level) == ((r_col >> level) ^ 1)))
        reach = (dot(s_pair, t_pair, NN) + eye).astype(BF)
        reach = jnp.where(reach > 0, 1.0, 0.0).astype(BF)
        for _ in range(max(1, bits_of(edges) - 1 - level)):
            reach = as_bf(dot(reach, reach, NN) > 0)
        mine = reach > 0
        partner = dot(s_pair, reach, NN) > 0
        first = lambda flag, ids, axis: jnp.min(jnp.where(flag, ids, edges), axis=axis, keepdims=True)
        bit_row = (first(mine, k_col, 0) < first(partner, k_col, 0)).astype(jnp.int32)
        bit_col = (first(mine, k_row, 1) < first(partner, k_row, 1)).astype(jnp.int32)
        c_row = c_row * 2 + bit_row
        c_col = c_col * 2 + bit_col
    return c_col, r_col[:, :1], k_col[:, :1]


def table_starts(groups, frames):
    starts = [0]
    for length in (frames, groups, frames, frames, groups, frames):
        starts.append(starts[-1] + length)
    return starts


def make_table(route_row, groups, frames, me):
    c, r, k = colour(route_row, groups, frames)
    shift = bits_of(frames)
    starts = table_starts(groups, frames)
    t = lax.broadcasted_iota(jnp.int32, (1, LANES), 1)
    source, target = k >> shift, r >> shift
    by_source, by_target = source * frames + c, target * frames + c
    via = me // 2
    runs = [
        (by_target, me * frames + t - starts[0], r & (frames - 1)),
        (by_source, (t - starts[1]) * frames + via, target),
        (k, me * frames + t - starts[2], c),
        (by_source, me * frames + t - starts[3], k & (frames - 1)),
        (by_target, (t - starts[4]) * frames + via, source),
        (r, me * frames + t - starts[5], c),
    ]
    table = jnp.zeros((1, LANES), jnp.int32)
    for i, (key, wanted, value) in enumerate(runs):
        found = jnp.sum(jnp.where(key == wanted, value, 0), axis=0, keepdims=True)
        found = jnp.clip(found, 0, starts[i + 1] - starts[i] - 1)
        table = jnp.where((t >= starts[i]) & (t < starts[i + 1]), found, table)
    return table


def kernel(
    groups,
    route,
    counts,
    route_row,
    lat,
    ct,
    mod,
    wqkv_hbm,
    wout_hbm,
    out_ref,
    grad_ref,
    wqkv,
    wout,
    c1_send,
    c1_recv,
    c2_send,
    c2_recv,
    o1_send,
    o1_recv,
    o2_send,
    o2_recv,
    ct_stage,
    ct_rows,
    out_stage,
    out_mid,
    grad_stage,
    mod_send,
    mod_recv,
    modf,
    x_rows,
    normed,
    qkv,
    qp,
    kp,
    vp,
    probs,
    op,
    att,
    dop,
    dk_own,
    dv_own,
    part_send,
    part_recv,
    tab_row,
    tab,
    w_sem,
    xs,
    xr,
    ms,
    mr,
    c1s,
    c1r,
    c2s,
    c2r,
    czs,
    czr,
    kvs,
    kvr,
    ozs,
    ozr,
    o1s,
    o1r,
    o2s,
    o2r,
    ps,
    pr,
    gs,
    gr,
):
    frames, rows, width = ct.shape
    head = width // HEADS
    zs = frames
    half = frames * rows
    me = lax.axis_index("grp")
    sp = lax.axis_index("sp")
    z = sp // 2
    core = sp % 2
    starts = table_starts(groups, frames)
    piece = rows // 2

    def z_dev(d):
        return {"sp": lax.rem(z + d, zs) * 2 + core}

    def g_dev(d):
        return {"grp": lax.rem(me + d, groups)}

    other = {"sp": z * 2 + (1 - core)}

    w1 = pltpu.make_async_copy(wqkv_hbm, wqkv, w_sem.at[0])
    w2 = pltpu.make_async_copy(wout_hbm, wout, w_sem.at[1])
    w1.start()
    w2.start()

    barrier = pltpu.get_barrier_semaphore()
    for d in range(1, zs):
        pl.semaphore_signal(barrier, inc=1, device_id=z_dev(d), device_id_type=MESH)
    for d in range(1, groups):
        pl.semaphore_signal(barrier, inc=1, device_id=g_dev(d), device_id_type=MESH)
    pl.semaphore_signal(barrier, inc=1, device_id=other, device_id_type=MESH)

    ends = [counts[0, 0]]
    for i in range(1, counts.shape[1] - 1):
        ends.append(ends[-1] + counts[0, i])
    for g in range(groups):
        slot = lax.rem(route[g * frames + z], frames)
        clip = sum([jnp.where(slot >= end, 1, 0) for end in ends])
        mod_send[g] = mod[clip]

    pl.semaphore_wait(barrier, zs - 1 + groups - 1 + 1)

    def remote(src, dst, s_sem, r_sem, dev):
        return pltpu.make_async_remote_copy(
            src_ref=src, dst_ref=dst, send_sem=s_sem, recv_sem=r_sem, device_id=dev, device_id_type=MESH
        )

    def group_copies(src, dst, s_sem, r_sem):
        own = pltpu.make_async_copy(src.at[me], dst.at[me], s_sem.at[0])
        return [own] + [
            remote(src.at[lax.rem(me + d, groups)], dst.at[me], s_sem.at[d], r_sem.at[d], g_dev(d))
            for d in range(1, groups)
        ]

    def z_copies(src, dst, s_sem, r_sem):
        own = pltpu.make_async_copy(src.at[z], dst.at[z], s_sem.at[0])
        return [own] + [
            remote(src.at[lax.rem(z + d, zs)], dst.at[z], s_sem.at[d], r_sem.at[d], z_dev(d))
            for d in range(1, zs)
        ]

    def start(copies):
        for copy in copies:
            copy.start()

    def wait_recv(copies):
        copies[0].wait()
        for copy in copies[1:]:
            copy.wait_recv()

    def wait_send(copies):
        for copy in copies[1:]:
            copy.wait_send()

    mod_c = group_copies(mod_send, mod_recv, ms, mr)
    x_c = z_copies(lat, x_rows, xs, xr)
    start(x_c)
    start(mod_c)

    tab_row[...] = make_table(route_row[...], groups, frames, me)
    tab_c = pltpu.make_async_copy(tab_row, tab, w_sem.at[2])
    tab_c.start()
    tab_c.wait()

    def spread_frames(source, first, send):
        for m in range(groups):
            send[m] = source[tab[0, first + m // 2], (m % 2) * piece : (m % 2 + 1) * piece, :]

    def pass_on(received, first, send):
        for g in range(groups):
            send[g] = received[tab[0, first + g]]

    def join_frames(received, first, target):
        for f in range(frames):
            c = tab[0, first + f]
            target[f, :piece, :] = received[2 * c]
            target[f, piece:, :] = received[2 * c + 1]

    spread_frames(ct, starts[0], c1_send)
    c1_c = group_copies(c1_send, c1_recv, c1s, c1r)
    start(c1_c)

    qkv[:, 3 * width :] = jnp.zeros((half, qkv.shape[1] - 3 * width), BF)
    wait_recv(mod_c)
    modf[:3, :] = mod_recv[route[me * frames + z] // frames]
    wait_recv(x_c)

    def norm_parts(r):
        x = x_rows[r].astype(F32)
        center = jnp.mean(x, axis=-1, keepdims=True)
        spread = x - center
        inv = lax.rsqrt(jnp.mean(spread * spread, axis=-1, keepdims=True) + EPS)
        return x, spread * inv, inv

    def norm_step(r, carry):
        _, xhat, _ = norm_parts(r)
        normed[pl.ds(r * rows, rows), :] = (xhat * (1.0 + modf[1:2, :]) + modf[0:1, :]).astype(BF)
        return carry

    lax.fori_loop(0, frames, norm_step, 0)

    wait_recv(c1_c)
    pass_on(c1_recv, starts[1], c2_send)
    c2_c = group_copies(c2_send, c2_recv, c2s, c2r)
    start(c2_c)

    w1.wait()
    lane = lax.broadcasted_iota(jnp.int32, (half, LANES), 1)

    def project(start_col, tile, count):
        def step(i, carry):
            cols = pl.ds(pl.multiple_of(start_col + i * tile, LANES), tile)
            qkv[:, cols] = dot(normed[...], wqkv[:, cols], NN).astype(BF)
            return carry

        lax.fori_loop(0, count, step, 0)

    def padded(source, start_col):
        piece = source[:, start_col : start_col + LANES]
        return jnp.where(lane < head, piece, jnp.zeros_like(piece))

    project(width, 256, 2 * width // 256)
    for h in range(HEADS):
        spot = slice(h * LANES, (h + 1) * LANES)
        kp[0, :, spot] = padded(qkv, width + h * head)
        vp[0, :, spot] = padded(qkv, 2 * width + h * head)
    k_c = remote(kp.at[0], kp.at[1], kvs.at[0], kvr.at[0], other)
    v_c = remote(vp.at[0], vp.at[1], kvs.at[1], kvr.at[1], other)
    k_c.start()
    v_c.start()
    project(0, 384, width // 384)
    for h in range(HEADS):
        qp[:, h * LANES : (h + 1) * LANES] = padded(qkv, h * head)
    k_c.wait_recv()
    v_c.wait_recv()

    factor = head**-0.5
    log2 = factor * math.log2(math.e)
    unroll = 2

    def spot_of(h):
        return pl.ds(pl.multiple_of(h * LANES, LANES), LANES)

    def forward_step(i, carry):
        for u in range(unroll):
            h = i * unroll + u
            spot = spot_of(h)
            k = kp[:, :, spot].reshape(2 * half, LANES)
            v = vp[:, :, spot].reshape(2 * half, LANES)
            scores = dot(k, qp[:, spot], NT)
            top = jnp.max(scores, axis=0, keepdims=True)
            ex = jnp.exp2((scores - top) * log2)
            p = (ex * (1.0 / jnp.sum(ex, axis=0, keepdims=True))).astype(BF)
            probs[h] = p
            op[:, spot] = dot(v, p, TN).T.astype(BF)
        return carry

    early = HEADS // unroll // 4
    lax.fori_loop(0, early, forward_step, 0)
    wait_recv(c2_c)
    join_frames(c2_recv, starts[2], ct_stage)
    cz_c = z_copies(ct_stage, ct_rows, czs, czr)
    start(cz_c)
    lax.fori_loop(early, HEADS // unroll, forward_step, 0)
    for h in range(HEADS):
        att[:, h * head : (h + 1) * head] = op[:, h * LANES : h * LANES + head]

    w2.wait()

    def out_step(i, carry):
        cols = pl.ds(pl.multiple_of(i * 384, LANES), 384)
        proj = dot(att[...], wout[:, cols], NN)
        x = x_rows[:, :, cols].reshape(half, 384).astype(F32)
        out_stage[:, :, cols] = (x + modf[2:3, cols] * proj).astype(BF).reshape(frames, rows, 384)
        return carry

    lax.fori_loop(0, width // 384, out_step, 0)
    oz_c = z_copies(out_stage, out_mid, ozs, ozr)
    start(oz_c)

    wait_recv(cz_c)

    def gated_step(r, carry):
        normed_rows = pl.ds(r * rows, rows)
        att[normed_rows, :] = (ct_rows[r].astype(F32) * modf[2:3, :]).astype(BF)
        return carry

    lax.fori_loop(0, frames, gated_step, 0)

    def back_out_step(i, carry):
        cols = pl.ds(pl.multiple_of(i * 384, LANES), 384)
        qkv[:, cols] = dot(att[...], wout[cols, :], NT).astype(BF)
        return carry

    lax.fori_loop(0, width // 384, back_out_step, 0)
    for h in range(HEADS):
        dop[:, h * LANES : (h + 1) * LANES] = padded(qkv, h * head)

    segments = part_send.shape[0]
    per = HEADS // segments

    def backward_step(seg, i, carry):
        for u in range(unroll):
            j = i * unroll + u
            h = seg * per + j
            spot = spot_of(h)
            k = kp[:, :, spot].reshape(2 * half, LANES)
            v = vp[:, :, spot].reshape(2 * half, LANES)
            do = dop[:, spot]
            p = probs[h]
            p_wide = p.astype(F32)
            weighted = p_wide * dot(v, do, NT)
            total = jnp.sum(weighted, axis=0, keepdims=True)
            ds = ((weighted - p_wide * total) * factor).astype(BF)
            dv = dot(p, do, NN)
            dk = dot(ds, qp[:, spot], NN)
            op[:, spot] = dot(k, ds, TN).T.astype(BF)
            dk_own[:, spot] = dk[:half]
            dv_own[:, spot] = dv[:half]
            part_send[seg, 0, :, spot_of(j)] = dk[half:].astype(BF)
            part_send[seg, 1, :, spot_of(j)] = dv[half:].astype(BF)
        return carry

    part_c = []
    for seg in range(segments):
        lax.fori_loop(0, per // unroll, functools.partial(backward_step, seg), 0)
        copy = remote(part_send.at[seg], part_recv.at[seg], ps.at[seg], pr.at[seg], other)
        copy.start()
        part_c.append(copy)
    for h in range(HEADS):
        qkv[:, h * head : (h + 1) * head] = op[:, h * LANES : h * LANES + head]
    for seg in range(segments):
        part_c[seg].wait_recv()
        for j in range(per):
            h = seg * per + j
            spot = slice(h * LANES, (h + 1) * LANES)
            there = slice(j * LANES, (j + 1) * LANES)
            dk = (dk_own[:, spot] + part_recv[seg, 0, :, there].astype(F32)).astype(BF)
            dv = (dv_own[:, spot] + part_recv[seg, 1, :, there].astype(F32)).astype(BF)
            qkv[:, width + h * head : width + (h + 1) * head] = dk[:, :head]
            qkv[:, 2 * width + h * head : 2 * width + (h + 1) * head] = dv[:, :head]

    def back_in_step(i, carry):
        cols = pl.ds(pl.multiple_of(i * 384, LANES), 384)
        att[:, cols] = dot(qkv[:, : 3 * width], wqkv[cols, :], NT).astype(BF)
        return carry

    lax.fori_loop(0, width // 384, back_in_step, 0)

    wait_recv(oz_c)
    spread_frames(out_mid, starts[3], o1_send)
    o1_c = group_copies(o1_send, o1_recv, o1s, o1r)
    start(o1_c)

    def grad_step(r, carry):
        _, xhat, inv = norm_parts(r)
        dhat = att[pl.ds(r * rows, rows), :].astype(F32) * (1.0 + modf[1:2, :])
        m1 = jnp.mean(dhat, axis=-1, keepdims=True)
        m2 = jnp.mean(dhat * xhat, axis=-1, keepdims=True)
        grad_stage[r] = (ct_rows[r].astype(F32) + inv * (dhat - m1 - xhat * m2)).astype(BF)
        return carry

    lax.fori_loop(0, frames, grad_step, 0)
    gz_c = z_copies(grad_stage, grad_ref, gs, gr)
    start(gz_c)

    wait_recv(o1_c)
    pass_on(o1_recv, starts[4], o2_send)
    o2_c = group_copies(o2_send, o2_recv, o2s, o2r)
    start(o2_c)
    wait_recv(gz_c)
    wait_recv(o2_c)
    join_frames(o2_recv, starts[5], out_ref)

    for copies in (mod_c, x_c, c1_c, c2_c, oz_c, cz_c, o1_c, o2_c, gz_c):
        wait_send(copies)
    k_c.wait_send()
    v_c.wait_send()
    for copy in part_c:
        copy.wait_send()


def local(latents, route, counts, modulation, w_qkv, w_out, cotangent):
    frames, rows, width = latents.shape
    groups = lax.axis_size("grp")
    half = frames * rows
    padded = HEADS * LANES
    segments = 4
    piece = (frames, rows, width)
    hop = (groups, rows // 2, width)
    dma = pltpu.SemaphoreType.DMA
    vmem = pltpu.VMEM
    block = jax.ShapeDtypeStruct(piece, BF)
    scratch = [vmem(w_qkv.shape, BF), vmem(w_out.shape, BF)]
    scratch += [vmem(hop, BF)] * 8
    scratch += [vmem(piece, BF)] * 5
    scratch += [vmem((groups, 3, width), F32)] * 2
    scratch += [
        vmem((8, width), F32),
        vmem(piece, BF),
        vmem((half, width), BF),
        vmem((half, 3 * width + LANES), BF),
        vmem((half, padded), BF),
        vmem((2, half, padded), BF),
        vmem((2, half, padded), BF),
        vmem((HEADS, 2 * half, half), BF),
        vmem((half, padded), BF),
        vmem((half, width), BF),
        vmem((half, padded), BF),
        vmem((half, padded), F32),
        vmem((half, padded), F32),
        vmem((segments, 2, half, padded // segments), BF),
        vmem((segments, 2, half, padded // segments), BF),
        vmem((1, LANES), jnp.int32),
        pltpu.SMEM((1, LANES), jnp.int32),
        dma((3,)),
    ]
    scratch += [dma((frames,))] * 2 + [dma((groups,))] * 6 + [dma((frames,))] * 2 + [dma((2,))] * 2
    scratch += [dma((frames,))] * 2 + [dma((groups,))] * 4 + [dma((segments,))] * 2 + [dma((frames,))] * 2
    in_vmem = pl.BlockSpec(memory_space=vmem)
    in_smem = pl.BlockSpec(memory_space=pltpu.SMEM)
    anywhere = pl.BlockSpec(memory_space=pl.ANY)
    return pl.pallas_call(
        functools.partial(kernel, groups),
        out_shape=(block, block),
        in_specs=[in_smem, in_smem, in_vmem, anywhere, in_vmem, in_vmem, anywhere, anywhere],
        out_specs=(in_vmem, in_vmem),
        scratch_shapes=scratch,
        compiler_params=pltpu.CompilerParams(
            collective_id=0, has_side_effects=True, vmem_limit_bytes=60 * 1024 * 1024
        ),
    )(route, counts, route.reshape(1, -1), latents, cotangent, modulation, w_qkv, w_out)


def solution(mesh):
    rows = P("grp", "sp", None)
    return jax.shard_map(
        local,
        mesh=mesh,
        in_specs=(rows, P(), P("grp", None), P("grp", None, None), P(), P(), rows),
        out_specs=(rows, rows),
        check_vma=False,
    )
```

```python
import functools
import math

import jax
import jax.numpy as jnp
from jax import lax
from jax.experimental import pallas as pl
from jax.experimental.pallas import tpu as pltpu
from jax.sharding import PartitionSpec as P

MESH = pl.DeviceIdType.MESH
HEADS = 16
LANES = 128
EPS = 1e-06
NT = (((1,), (1,)), ((), ()))
NN = (((1,), (0,)), ((), ()))
TN = (((0,), (0,)), ((), ()))
BF = jnp.bfloat16
F32 = jnp.float32


def dot(a, b, dims):
    return lax.dot_general(a, b, dims, preferred_element_type=F32)


def bits_of(number):
    return number.bit_length() - 1


def colour(route_row, groups, frames):
    edges = groups * frames
    shift = bits_of(frames)
    square = (edges, edges)
    r_wide = jnp.broadcast_to(route_row.astype(F32), square)
    r_row, r_col = r_wide.astype(jnp.int32), r_wide.T.astype(jnp.int32)
    k_row = lax.broadcasted_iota(jnp.int32, square, 1)
    k_col = lax.broadcasted_iota(jnp.int32, square, 0)
    same_source = (k_row >> shift) == (k_col >> shift)
    same_target = (r_row >> shift) == (r_col >> shift)
    as_bf = lambda flag: jnp.where(flag, 1.0, 0.0).astype(BF)
    eye = jnp.where(k_row == k_col, 1.0, 0.0)
    c_row = jnp.zeros((1, edges), jnp.int32)
    c_col = jnp.zeros((edges, 1), jnp.int32)
    for level in range(shift):
        same = c_row == c_col
        s_pair = as_bf(same & same_source & ((k_row >> level) == ((k_col >> level) ^ 1)))
        t_pair = as_bf(same & same_target & ((r_row >> level) == ((r_col >> level) ^ 1)))
        reach = (dot(s_pair, t_pair, NN) + eye).astype(BF)
        reach = jnp.where(reach > 0, 1.0, 0.0).astype(BF)
        for _ in range(max(1, bits_of(edges) - 1 - level)):
            reach = as_bf(dot(reach, reach, NN) > 0)
        mine = reach > 0
        partner = dot(s_pair, reach, NN) > 0
        first = lambda flag, ids, axis: jnp.min(jnp.where(flag, ids, edges), axis=axis, keepdims=True)
        bit_row = (first(mine, k_col, 0) < first(partner, k_col, 0)).astype(jnp.int32)
        bit_col = (first(mine, k_row, 1) < first(partner, k_row, 1)).astype(jnp.int32)
        c_row = c_row * 2 + bit_row
        c_col = c_col * 2 + bit_col
    return c_col, r_col[:, :1], k_col[:, :1]


def table_starts(groups, frames):
    starts = [0]
    for length in (frames, groups, frames, frames, groups, frames):
        starts.append(starts[-1] + length)
    return starts


def make_table(route_row, groups, frames, me):
    c, r, k = colour(route_row, groups, frames)
    shift = bits_of(frames)
    starts = table_starts(groups, frames)
    t = lax.broadcasted_iota(jnp.int32, (1, LANES), 1)
    source, target = k >> shift, r >> shift
    by_source, by_target = source * frames + c, target * frames + c
    via = me // 2
    runs = [
        (by_target, me * frames + t - starts[0], r & (frames - 1)),
        (by_source, (t - starts[1]) * frames + via, target),
        (k, me * frames + t - starts[2], c),
        (by_source, me * frames + t - starts[3], k & (frames - 1)),
        (by_target, (t - starts[4]) * frames + via, source),
        (r, me * frames + t - starts[5], c),
    ]
    table = jnp.zeros((1, LANES), jnp.int32)
    for i, (key, wanted, value) in enumerate(runs):
        found = jnp.sum(jnp.where(key == wanted, value, 0), axis=0, keepdims=True)
        found = jnp.clip(found, 0, starts[i + 1] - starts[i] - 1)
        table = jnp.where((t >= starts[i]) & (t < starts[i + 1]), found, table)
    return table


def kernel(
    groups,
    route,
    counts,
    route_row,
    lat,
    ct,
    mod,
    wqkv_hbm,
    wout_hbm,
    out_ref,
    grad_ref,
    wqkv,
    wout,
    c1_send,
    c1_recv,
    c2_send,
    c2_recv,
    o1_send,
    o1_recv,
    o2_send,
    o2_recv,
    ct_stage,
    ct_rows,
    out_stage,
    out_mid,
    grad_stage,
    mod_send,
    mod_recv,
    modf,
    x_rows,
    normed,
    qkv,
    qp,
    kp,
    vp,
    probs,
    op,
    att,
    dop,
    dk_own,
    dv_own,
    part_send,
    part_recv,
    tab_row,
    tab,
    w_sem,
    xs,
    xr,
    ms,
    mr,
    c1s,
    c1r,
    c2s,
    c2r,
    czs,
    czr,
    kvs,
    kvr,
    ozs,
    ozr,
    o1s,
    o1r,
    o2s,
    o2r,
    ps,
    pr,
    gs,
    gr,
):
    frames, rows, width = ct.shape
    head = width // HEADS
    zs = frames
    half = frames * rows
    me = lax.axis_index("grp")
    sp = lax.axis_index("sp")
    z = sp // 2
    core = sp % 2
    starts = table_starts(groups, frames)
    piece = rows // 2

    def z_dev(d):
        return {"sp": lax.rem(z + d, zs) * 2 + core}

    def g_dev(d):
        return {"grp": lax.rem(me + d, groups)}

    other = {"sp": z * 2 + (1 - core)}

    w1 = pltpu.make_async_copy(wqkv_hbm, wqkv, w_sem.at[0])
    w2 = pltpu.make_async_copy(wout_hbm, wout, w_sem.at[1])
    w1.start()
    w2.start()

    barrier = pltpu.get_barrier_semaphore()
    for d in range(1, zs):
        pl.semaphore_signal(barrier, inc=1, device_id=z_dev(d), device_id_type=MESH)
    for d in range(1, groups):
        pl.semaphore_signal(barrier, inc=1, device_id=g_dev(d), device_id_type=MESH)
    pl.semaphore_signal(barrier, inc=1, device_id=other, device_id_type=MESH)

    def remote(src, dst, s_sem, r_sem, dev):
        return pltpu.make_async_remote_copy(
            src_ref=src, dst_ref=dst, send_sem=s_sem, recv_sem=r_sem, device_id=dev, device_id_type=MESH
        )

    def group_copies(src, dst, s_sem, r_sem):
        own = pltpu.make_async_copy(src.at[me], dst.at[me], s_sem.at[0])
        return [own] + [
            remote(src.at[lax.rem(me + d, groups)], dst.at[me], s_sem.at[d], r_sem.at[d], g_dev(d))
            for d in range(1, groups)
        ]

    near_first = sorted(range(1, zs), key=lambda d: min(d, zs - d))

    def to_frames(src, dst, s_sem, r_sem):
        own = pltpu.make_async_copy(src.at[z], dst.at[0], s_sem.at[0])
        return [own] + [
            remote(src.at[lax.rem(z + d, zs)], dst.at[zs - d], s_sem.at[d], r_sem.at[d], z_dev(d)) for d in near_first
        ]

    def from_frames(src, dst, s_sem, r_sem):
        own = pltpu.make_async_copy(src.at[0], dst.at[z], s_sem.at[0])
        return [own] + [
            remote(src.at[d], dst.at[z], s_sem.at[d], r_sem.at[d], z_dev(d)) for d in near_first
        ]

    def start(copies):
        for copy in copies:
            copy.start()

    def wait_recv(copies):
        copies[0].wait()
        for copy in copies[1:]:
            copy.wait_recv()

    def wait_send(copies):
        for copy in copies[1:]:
            copy.wait_send()

    tab_row[...] = make_table(route_row[...], groups, frames, me)
    tab_c = pltpu.make_async_copy(tab_row, tab, w_sem.at[2])
    tab_c.start()

    ends = [counts[0, 0]]
    for i in range(1, counts.shape[1] - 1):
        ends.append(ends[-1] + counts[0, i])
    for g in range(groups):
        slot = lax.rem(route[g * frames + z], frames)
        clip = sum([jnp.where(slot >= end, 1, 0) for end in ends])
        for i in range(3):
            mod_send[g, i : i + 1, :] = mod[i, pl.ds(clip, 1), :]

    tab_c.wait()

    def spread_frames(source, first, send):
        for m in range(groups):
            send[m] = source[tab[0, first + m // 2], (m % 2) * piece : (m % 2 + 1) * piece, :]

    def pass_on(received, first, send):
        for g in range(groups):
            send[g] = received[tab[0, first + g]]

    def join_frames(received, first, target):
        for f in range(frames):
            c = tab[0, first + f]
            target[f, :piece, :] = received[2 * c]
            target[f, piece:, :] = received[2 * c + 1]

    spread_frames(ct, starts[0], c1_send)
    pl.semaphore_wait(barrier, zs - 1 + groups - 1 + 1)

    x_c = to_frames(lat, x_rows, xs, xr)
    c1_c = group_copies(c1_send, c1_recv, c1s, c1r)
    mod_c = group_copies(mod_send, mod_recv, ms, mr)
    start(x_c)
    start(c1_c)
    start(mod_c)

    qkv[:, 3 * width :] = jnp.zeros((half, qkv.shape[1] - 3 * width), BF)
    wait_recv(c1_c)
    pass_on(c1_recv, starts[1], c2_send)
    c2_c = group_copies(c2_send, c2_recv, c2s, c2r)
    start(c2_c)
    wait_recv(mod_c)
    modf[:3, :] = mod_recv[route[me * frames + z] // frames]

    def norm_parts(r):
        x = x_rows[r].astype(F32)
        center = jnp.mean(x, axis=-1, keepdims=True)
        spread = x - center
        inv = lax.rsqrt(jnp.mean(spread * spread, axis=-1, keepdims=True) + EPS)
        return x, spread * inv, inv

    for i, r in enumerate([0] + [zs - d for d in near_first]):
        x_c[i].wait() if i == 0 else x_c[i].wait_recv()
        _, xhat, _ = norm_parts(r)
        normed[r * rows : (r + 1) * rows, :] = (xhat * (1.0 + modf[1:2, :]) + modf[0:1, :]).astype(BF)

    w1.wait()
    lane = lax.broadcasted_iota(jnp.int32, (half, LANES), 1)

    def project(start_col, tile, count):
        def step(i, carry):
            cols = pl.ds(pl.multiple_of(start_col + i * tile, LANES), tile)
            qkv[:, cols] = dot(normed[...], wqkv[:, cols], NN).astype(BF)
            return carry

        lax.fori_loop(0, count, step, 0)

    def padded(source, start_col):
        piece = source[:, start_col : start_col + LANES]
        return jnp.where(lane < head, piece, jnp.zeros_like(piece))

    k_c = remote(kp.at[0], kp.at[1], kvs.at[0], kvr.at[0], other)
    v_c = remote(vp.at[0], vp.at[1], kvs.at[1], kvr.at[1], other)
    tiles = 2 * width // 256
    k_tiles = -(-width // 256)
    project(width, 256, k_tiles)
    for h in range(HEADS):
        kp[0, :, h * LANES : (h + 1) * LANES] = padded(qkv, width + h * head)
    k_c.start()
    wait_recv(c2_c)
    join_frames(c2_recv, starts[2], ct_stage)
    cz_c = to_frames(ct_stage, ct_rows, czs, czr)
    start(cz_c)
    project(width + k_tiles * 256, 256, tiles - k_tiles)
    for h in range(HEADS):
        vp[0, :, h * LANES : (h + 1) * LANES] = padded(qkv, 2 * width + h * head)
    v_c.start()
    project(0, 384, width // 384)
    for h in range(HEADS):
        qp[:, h * LANES : (h + 1) * LANES] = padded(qkv, h * head)
    k_c.wait_recv()
    v_c.wait_recv()

    factor = head**-0.5
    log2 = factor * math.log2(math.e)
    unroll = 4

    def spot_of(h):
        return pl.ds(pl.multiple_of(h * LANES, LANES), LANES)

    def forward_step(i, carry):
        for u in range(unroll):
            h = i * unroll + u
            spot = spot_of(h)
            k = kp[:, :, spot].reshape(2 * half, LANES)
            v = vp[:, :, spot].reshape(2 * half, LANES)
            scores = dot(k, qp[:, spot], NT)
            top = jnp.max(scores, axis=0, keepdims=True)
            ex = jnp.exp2((scores - top) * log2)
            p = (ex * (1.0 / jnp.sum(ex, axis=0, keepdims=True))).astype(BF)
            probs[h] = p
            op[:, spot] = dot(v, p, TN).T.astype(BF)
        return carry

    lax.fori_loop(0, HEADS // unroll, forward_step, 0)
    for h in range(HEADS):
        att[:, h * head : (h + 1) * head] = op[:, h * LANES : h * LANES + head]

    w2.wait()

    def out_step(i, carry):
        cols = pl.ds(pl.multiple_of(i * 384, LANES), 384)
        proj = dot(att[...], wout[:, cols], NN)
        x = x_rows[:, :, cols].reshape(half, 384).astype(F32)
        out_stage[:, :, cols] = (x + modf[2:3, cols] * proj).astype(BF).reshape(frames, rows, 384)
        return carry

    lax.fori_loop(0, width // 384, out_step, 0)
    wait_recv(cz_c)
    oz_c = from_frames(out_stage, out_mid, ozs, ozr)
    start(oz_c)

    def gated_step(r, carry):
        normed_rows = pl.ds(r * rows, rows)
        att[normed_rows, :] = (ct_rows[r].astype(F32) * modf[2:3, :]).astype(BF)
        return carry

    lax.fori_loop(0, frames, gated_step, 0)

    def back_out_step(i, carry):
        cols = pl.ds(pl.multiple_of(i * 384, LANES), 384)
        qkv[:, cols] = dot(att[...], wout[cols, :], NT).astype(BF)
        return carry

    lax.fori_loop(0, width // 384, back_out_step, 0)
    for h in range(HEADS):
        dop[:, h * LANES : (h + 1) * LANES] = padded(qkv, h * head)

    segments = part_send.shape[0]
    per = HEADS // segments

    def backward_step(seg, i, carry):
        for u in range(unroll):
            j = i * unroll + u
            h = seg * per + j
            spot = spot_of(h)
            k = kp[:, :, spot].reshape(2 * half, LANES)
            v = vp[:, :, spot].reshape(2 * half, LANES)
            do = dop[:, spot]
            p = probs[h]
            p_wide = p.astype(F32)
            weighted = p_wide * dot(v, do, NT)
            total = jnp.sum(weighted, axis=0, keepdims=True)
            ds = ((weighted - p_wide * total) * factor).astype(BF)
            dv = dot(p, do, NN)
            dk = dot(ds, qp[:, spot], NN)
            op[:, spot] = dot(k, ds, TN).T.astype(BF)
            dk_own[:, spot] = dk[:half]
            dv_own[:, spot] = dv[:half]
            part_send[seg, 0, :, spot_of(j)] = dk[half:].astype(BF)
            part_send[seg, 1, :, spot_of(j)] = dv[half:].astype(BF)
        return carry

    part_c = []
    for seg in range(segments):
        lax.fori_loop(0, per // unroll, functools.partial(backward_step, seg), 0)
        copy = remote(part_send.at[seg], part_recv.at[seg], ps.at[seg], pr.at[seg], other)
        copy.start()
        part_c.append(copy)
    for h in range(HEADS):
        qkv[:, h * head : (h + 1) * head] = op[:, h * LANES : h * LANES + head]
    for seg in range(segments):
        part_c[seg].wait_recv()
        for j in range(per):
            h = seg * per + j
            spot = slice(h * LANES, (h + 1) * LANES)
            there = slice(j * LANES, (j + 1) * LANES)
            dk = (dk_own[:, spot] + part_recv[seg, 0, :, there].astype(F32)).astype(BF)
            dv = (dv_own[:, spot] + part_recv[seg, 1, :, there].astype(F32)).astype(BF)
            qkv[:, width + h * head : width + (h + 1) * head] = dk[:, :head]
            qkv[:, 2 * width + h * head : 2 * width + (h + 1) * head] = dv[:, :head]

    def back_in_step(i, carry):
        cols = pl.ds(pl.multiple_of(i * 384, LANES), 384)
        att[:, cols] = dot(qkv[:, : 3 * width], wqkv[cols, :], NT).astype(BF)
        return carry

    lax.fori_loop(0, width // 384, back_in_step, 0)

    wait_recv(oz_c)
    spread_frames(out_mid, starts[3], o1_send)
    o1_c = group_copies(o1_send, o1_recv, o1s, o1r)
    start(o1_c)

    gz_c = from_frames(grad_stage, grad_ref, gs, gr)
    for i, r in enumerate([0] + near_first):
        _, xhat, inv = norm_parts(r)
        dhat = att[r * rows : (r + 1) * rows, :].astype(F32) * (1.0 + modf[1:2, :])
        m1 = jnp.mean(dhat, axis=-1, keepdims=True)
        m2 = jnp.mean(dhat * xhat, axis=-1, keepdims=True)
        grad_stage[r] = (ct_rows[r].astype(F32) + inv * (dhat - m1 - xhat * m2)).astype(BF)
        gz_c[i].start()

    wait_recv(o1_c)
    pass_on(o1_recv, starts[4], o2_send)
    o2_c = group_copies(o2_send, o2_recv, o2s, o2r)
    start(o2_c)
    wait_recv(gz_c)
    wait_recv(o2_c)
    join_frames(o2_recv, starts[5], out_ref)

    for copies in (mod_c, x_c, c1_c, c2_c, oz_c, cz_c, o1_c, o2_c, gz_c):
        wait_send(copies)
    k_c.wait_send()
    v_c.wait_send()
    for copy in part_c:
        copy.wait_send()


def place(out_from, grad_from, out_ref, grad_ref):
    out_ref[...] = out_from[...]
    grad_ref[...] = grad_from[...]


def local(latents, route, counts, modulation, w_qkv, w_out, cotangent):
    frames, rows, width = latents.shape
    groups = lax.axis_size("grp")
    half = frames * rows
    padded = HEADS * LANES
    segments = 4
    piece = (frames, rows, width)
    hop = (groups, rows // 2, width)
    dma = pltpu.SemaphoreType.DMA
    vmem = pltpu.VMEM
    block = jax.ShapeDtypeStruct(piece, BF)
    scratch = [vmem(w_qkv.shape, BF), vmem(w_out.shape, BF)]
    scratch += [vmem(hop, BF)] * 8
    scratch += [vmem(piece, BF)] * 5
    scratch += [vmem((groups, 3, width), F32)] * 2
    scratch += [
        vmem((8, width), F32),
        vmem(piece, BF),
        vmem((half, width), BF),
        vmem((half, 3 * width + LANES), BF),
        vmem((half, padded), BF),
        vmem((2, half, padded), BF),
        vmem((2, half, padded), BF),
        vmem((HEADS, 2 * half, half), BF),
        vmem((half, padded), BF),
        vmem((half, width), BF),
        vmem((half, padded), BF),
        vmem((half, padded), F32),
        vmem((half, padded), F32),
        vmem((segments, 2, half, padded // segments), BF),
        vmem((segments, 2, half, padded // segments), BF),
        vmem((1, LANES), jnp.int32),
        pltpu.SMEM((1, LANES), jnp.int32),
        dma((3,)),
    ]
    scratch += [dma((frames,))] * 2 + [dma((groups,))] * 6 + [dma((frames,))] * 2 + [dma((2,))] * 2
    scratch += [dma((frames,))] * 2 + [dma((groups,))] * 4 + [dma((segments,))] * 2 + [dma((frames,))] * 2
    in_vmem = pl.BlockSpec(memory_space=vmem)
    in_smem = pl.BlockSpec(memory_space=pltpu.SMEM)
    anywhere = pl.BlockSpec(memory_space=pl.ANY)
    results = pl.pallas_call(
        functools.partial(kernel, groups),
        out_shape=(block, block),
        in_specs=[in_smem, in_smem, in_vmem, anywhere, in_vmem, in_vmem, anywhere, anywhere],
        out_specs=(in_vmem, in_vmem),
        scratch_shapes=scratch,
        compiler_params=pltpu.CompilerParams(
            collective_id=0, has_side_effects=True, vmem_limit_bytes=60 * 1024 * 1024
        ),
    )(route, counts, route.reshape(1, -1), latents, cotangent, modulation.transpose(1, 0, 2), w_qkv, w_out)
    some = pl.BlockSpec((2, rows, width), lambda i: (i, 0, 0))
    return pl.pallas_call(
        place,
        out_shape=(block, block),
        grid=(frames // 2,),
        in_specs=[some, some],
        out_specs=(some, some),
    )(*results)


def solution(mesh):
    rows = P("grp", "sp", None)
    return jax.shard_map(
        local,
        mesh=mesh,
        in_specs=(rows, P(), P("grp", None), P("grp", None, None), P(), P(), rows),
        out_specs=(rows, rows),
        check_vma=False,
    )
```

```python
import functools
import math

import jax
import jax.numpy as jnp
from jax import lax
from jax.experimental import pallas as pl
from jax.experimental.pallas import tpu as pltpu
from jax.sharding import PartitionSpec as P

MESH = pl.DeviceIdType.MESH
HEADS = 16
LANES = 128
EPS = 1e-06
NT = (((1,), (1,)), ((), ()))
NN = (((1,), (0,)), ((), ()))
TN = (((0,), (0,)), ((), ()))
BF = jnp.bfloat16
F32 = jnp.float32


def dot(a, b, dims):
    return lax.dot_general(a, b, dims, preferred_element_type=F32)


def bits_of(number):
    return number.bit_length() - 1


def colour(route_row, groups, frames):
    edges = groups * frames
    shift = bits_of(frames)
    square = (edges, edges)
    r_wide = jnp.broadcast_to(route_row.astype(F32), square)
    r_row, r_col = r_wide.astype(jnp.int32), r_wide.T.astype(jnp.int32)
    k_row = lax.broadcasted_iota(jnp.int32, square, 1)
    k_col = lax.broadcasted_iota(jnp.int32, square, 0)
    same_source = (k_row >> shift) == (k_col >> shift)
    same_target = (r_row >> shift) == (r_col >> shift)
    as_bf = lambda flag: jnp.where(flag, 1.0, 0.0).astype(BF)
    eye = jnp.where(k_row == k_col, 1.0, 0.0)
    c_row = jnp.zeros((1, edges), jnp.int32)
    c_col = jnp.zeros((edges, 1), jnp.int32)
    for level in range(shift):
        same = c_row == c_col
        s_pair = as_bf(same & same_source & ((k_row >> level) == ((k_col >> level) ^ 1)))
        t_pair = as_bf(same & same_target & ((r_row >> level) == ((r_col >> level) ^ 1)))
        reach = (dot(s_pair, t_pair, NN) + dot(t_pair, s_pair, NN) + eye).astype(BF)
        for _ in range(max(1, bits_of(edges) - 2 - level)):
            reach = dot(reach, reach, NN).astype(BF)
        mine = reach > 0
        partner = dot(s_pair, reach, NN) > 0
        first = lambda flag, ids, axis: jnp.min(jnp.where(flag, ids, edges), axis=axis, keepdims=True)
        bit_row = (first(mine, k_col, 0) < first(partner, k_col, 0)).astype(jnp.int32)
        bit_col = (first(mine, k_row, 1) < first(partner, k_row, 1)).astype(jnp.int32)
        c_row = c_row * 2 + bit_row
        c_col = c_col * 2 + bit_col
    return c_col, r_col[:, :1], k_col[:, :1]


def table_starts(groups, frames):
    starts = [0]
    for length in (frames, groups, frames, frames, groups, frames):
        starts.append(starts[-1] + length)
    return starts


def make_table(route_row, groups, frames, me):
    c, r, k = colour(route_row, groups, frames)
    shift = bits_of(frames)
    starts = table_starts(groups, frames)
    t = lax.broadcasted_iota(jnp.int32, (1, LANES), 1)
    source, target = k >> shift, r >> shift
    by_source, by_target = source * frames + c, target * frames + c
    via = me // 2
    runs = [
        (by_target, me * frames + t - starts[0], r & (frames - 1)),
        (by_source, (t - starts[1]) * frames + via, target),
        (k, me * frames + t - starts[2], c),
        (by_source, me * frames + t - starts[3], k & (frames - 1)),
        (by_target, (t - starts[4]) * frames + via, source),
        (r, me * frames + t - starts[5], c),
    ]
    table = jnp.zeros((1, LANES), jnp.int32)
    for i, (key, wanted, value) in enumerate(runs):
        found = jnp.sum(jnp.where(key == wanted, value, 0), axis=0, keepdims=True)
        found = jnp.clip(found, 0, starts[i + 1] - starts[i] - 1)
        table = jnp.where((t >= starts[i]) & (t < starts[i + 1]), found, table)
    return table


def kernel(
    groups,
    route,
    counts,
    route_row,
    lat,
    ct_hbm,
    mod,
    wqkv_hbm,
    wout_hbm,
    out_ref,
    grad_ref,
    wqkv,
    wout,
    ct,
    c1_send,
    c1_recv,
    c2_send,
    c2_recv,
    o1_send,
    o1_recv,
    o2_send,
    o2_recv,
    ct_stage,
    ct_rows,
    out_stage,
    out_mid,
    grad_stage,
    mod_send,
    mod_recv,
    modf,
    x_rows,
    normed,
    qkv,
    qp,
    kp,
    vp,
    probs,
    op,
    att,
    dop,
    inverse,
    dk_own,
    dv_own,
    part_send,
    part_recv,
    tab_row,
    tab,
    w_sem,
    xs,
    xr,
    ms,
    mr,
    c1s,
    c1r,
    c2s,
    c2r,
    czs,
    czr,
    kvs,
    kvr,
    ozs,
    ozr,
    o1s,
    o1r,
    o2s,
    o2r,
    ps,
    pr,
    gs,
    gr,
):
    frames, rows, width = ct_hbm.shape
    head = width // HEADS
    zs = frames
    half = frames * rows
    me = lax.axis_index("grp")
    sp = lax.axis_index("sp")
    z = sp // 2
    core = sp % 2
    starts = table_starts(groups, frames)
    piece = rows // 2

    def z_dev(d):
        return {"sp": lax.rem(z + d, zs) * 2 + core}

    def g_dev(d):
        return {"grp": lax.rem(me + d, groups)}

    other = {"sp": z * 2 + (1 - core)}

    w1 = pltpu.make_async_copy(wqkv_hbm, wqkv, w_sem.at[0])
    w2 = pltpu.make_async_copy(wout_hbm, wout, w_sem.at[1])
    barrier = pltpu.get_barrier_semaphore()
    for d in range(1, zs):
        pl.semaphore_signal(barrier, inc=1, device_id=z_dev(d), device_id_type=MESH)
    for d in range(1, groups):
        pl.semaphore_signal(barrier, inc=1, device_id=g_dev(d), device_id_type=MESH)
    pl.semaphore_signal(barrier, inc=1, device_id=other, device_id_type=MESH)
    ct_c = pltpu.make_async_copy(ct_hbm, ct, w_sem.at[3])
    ct_c.start()
    w1.start()
    w2.start()

    def remote(src, dst, s_sem, r_sem, dev):
        return pltpu.make_async_remote_copy(
            src_ref=src, dst_ref=dst, send_sem=s_sem, recv_sem=r_sem, device_id=dev, device_id_type=MESH
        )

    middle = -(-width // LANES // 2) * LANES
    parts = [pl.ds(0, middle), pl.ds(middle, width - middle)]

    def group_copies(src, dst, s_sem, r_sem):
        def copies(i):
            own = pltpu.make_async_copy(src[i].at[me], dst[i].at[me], s_sem.at[i, 0])
            return [own] + [
                remote(src[i].at[lax.rem(me + d, groups)], dst[i].at[me], s_sem.at[i, d], r_sem.at[i, d], g_dev(d))
                for d in range(1, groups)
            ]

        return [copies(i) for i in range(2)]

    def mod_copies():
        own = pltpu.make_async_copy(mod_send.at[me], mod_recv.at[me], ms.at[0])
        return [own] + [
            remote(mod_send.at[lax.rem(me + d, groups)], mod_recv.at[me], ms.at[d], mr.at[d], g_dev(d))
            for d in range(1, groups)
        ]

    near_first = sorted(range(1, zs), key=lambda d: min(d, zs - d))

    ahead = [0] + [zs - d for d in near_first]

    def to_frames(src, dst, s_sem, r_sem, i, cols):
        own = pltpu.make_async_copy(src.at[z, :, cols], dst.at[0, :, cols], s_sem.at[i, 0])
        return [own] + [
            remote(
                src.at[lax.rem(z + d, zs), :, cols],
                dst.at[n + 1, :, cols],
                s_sem.at[i, d],
                r_sem.at[i, d],
                z_dev(d),
            )
            for n, d in enumerate(near_first)
        ]

    def from_frames(src, dst, s_sem, r_sem, i, cols):
        own = pltpu.make_async_copy(src.at[0, :, cols], dst.at[z], s_sem.at[i, 0])
        return [own] + [
            remote(src.at[n, :, cols], dst.at[z], s_sem.at[i, d], r_sem.at[i, d], z_dev(d))
            for n, d in list(enumerate(ahead))[1:]
        ]

    def start(copies):
        for copy in copies:
            copy.start()

    def wait_recv(copies):
        copies[0].wait()
        for copy in copies[1:]:
            copy.wait_recv()

    def wait_send(copies):
        for copy in copies[1:]:
            copy.wait_send()

    whole = pl.ds(0, width)
    tab_row[...] = make_table(route_row[...], groups, frames, me)
    tab_c = pltpu.make_async_copy(tab_row, tab, w_sem.at[2])
    tab_c.start()

    ends = [counts[0, 0]]
    for i in range(1, counts.shape[1] - 1):
        ends.append(ends[-1] + counts[0, i])
    for g in range(groups):
        slot = lax.rem(route[g * frames + z], frames)
        clip = sum([jnp.where(slot >= end, 1, 0) for end in ends])
        for i in range(3):
            mod_send[g, i : i + 1, :] = mod[i, pl.ds(clip, 1), :]

    tab_c.wait()
    ct_c.wait()

    def spread_frames(source, first, send, cols):
        for m in range(groups):
            send[m] = source[tab[0, first + m // 2], (m % 2) * piece : (m % 2 + 1) * piece, cols]

    def pass_on(received, first, send):
        for g in range(groups):
            send[g] = received[tab[0, first + g]]

    def join_frames(received, first, target, cols):
        for f in range(frames):
            c = tab[0, first + f]
            target[f, :piece, cols] = received[2 * c]
            target[f, piece:, cols] = received[2 * c + 1]

    for i, cols in enumerate(parts):
        spread_frames(ct, starts[0], c1_send[i], cols)
    pl.semaphore_wait(barrier, zs - 1 + groups - 1 + 1)

    x_c = to_frames(lat, x_rows, xs, xr, 0, whole)
    start(x_c)
    c1_c = group_copies(c1_send, c1_recv, c1s, c1r)
    c2_c = group_copies(c2_send, c2_recv, c2s, c2r)
    cz_c = [to_frames(ct_stage, ct_rows, czs, czr, i, cols) for i, cols in enumerate(parts)]
    mod_c = mod_copies()
    start(c1_c[0])
    start(c1_c[1])
    start(mod_c)

    def cotangent_on(i):
        wait_recv(c2_c[i])
        join_frames(c2_recv[i], starts[2], ct_stage, parts[i])
        start(cz_c[i])

    qkv[:, 3 * width :] = jnp.zeros((half, qkv.shape[1] - 3 * width), BF)
    for i in range(2):
        wait_recv(c1_c[i])
        pass_on(c1_recv[i], starts[1], c2_send[i])
        start(c2_c[i])
    wait_recv(mod_c)
    modf[:3, :] = mod_recv[route[me * frames + z] // frames]

    def norm_parts(r):
        x = x_rows[r].astype(F32)
        center = jnp.mean(x, axis=-1, keepdims=True)
        spread = x - center
        inv = lax.rsqrt(jnp.mean(spread * spread, axis=-1, keepdims=True) + EPS)
        return x, spread * inv, inv

    lane = lax.broadcasted_iota(jnp.int32, (half, LANES), 1)

    def arrive(first, last):
        for r in range(first, last):
            x_c[r].wait() if r == 0 else x_c[r].wait_recv()
            _, xhat, _ = norm_parts(r)
            normed[r * rows : (r + 1) * rows, :] = (xhat * (1.0 + modf[1:2, :]) + modf[0:1, :]).astype(BF)

    def project(start_col, stop_col, some):
        for at in range(start_col, stop_col, 256):
            cols = slice(at, min(at + 256, stop_col))
            qkv[some, cols] = dot(normed[some, :], wqkv[:, cols], NN).astype(BF)

    def padded(source, start_col):
        piece = source[:, start_col : start_col + LANES]
        return jnp.where(lane < head, piece, jnp.zeros_like(piece))

    k_c = remote(kp.at[0], kp.at[1], kvs.at[0], kvr.at[0], other)
    v_c = remote(vp.at[0], vp.at[1], kvs.at[1], kvr.at[1], other)
    k_stop = width + -(-width // 256) * 256
    arrive(0, zs // 2)
    w1.wait()
    early, late = slice(0, half // 2), slice(half // 2, half)
    project(width, 3 * width, early)
    project(0, width, early)
    cotangent_on(0)
    arrive(zs // 2, zs)
    project(width, k_stop, late)
    for h in range(HEADS):
        kp[0, :, h * LANES : (h + 1) * LANES] = padded(qkv, width + h * head)
    k_c.start()
    cotangent_on(1)
    project(k_stop, 3 * width, late)
    for h in range(HEADS):
        piece_v = padded(qkv, 2 * width + h * head)
        vp[0, :, h * LANES : (h + 1) * LANES] = jnp.where(lane == head, jnp.ones_like(piece_v), piece_v)
    v_c.start()
    project(0, width, late)
    for h in range(HEADS):
        qp[:, h * LANES : (h + 1) * LANES] = padded(qkv, h * head)
    k_c.wait_recv()
    v_c.wait_recv()

    factor = head**-0.5
    log2 = factor * math.log2(math.e)
    def spot_of(h):
        return pl.ds(h * LANES, LANES)

    def head_keys(ref, h):
        return ref[:, :, spot_of(h)].reshape(2 * half, LANES)

    def scores_of(h):
        return dot(head_keys(kp, h), qp[:, spot_of(h)], NT)

    def attend(h, scores):
        top = jnp.max(scores, axis=0, keepdims=True)
        ex = jnp.exp2((scores - top) * log2).astype(BF)
        probs[h] = ex
        mixed = dot(head_keys(vp, h), ex, TN).T
        inv = 1.0 / mixed[:, head : head + 1]
        inverse[h] = jnp.broadcast_to(inv, (half, LANES))
        op[:, spot_of(h)] = (mixed * inv).astype(BF)

    scores = scores_of(0)
    for h in range(HEADS):
        upcoming = scores_of(h + 1) if h + 1 < HEADS else None
        attend(h, scores)
        scores = upcoming

    for h in range(HEADS):
        att[:, h * head : (h + 1) * head] = op[:, h * LANES : h * LANES + head]

    w2.wait()

    col_tiles = [slice(at, min(at + 256, width)) for at in range(0, width, 256)]
    for cols in col_tiles:
        proj = dot(att[...], wout[:, cols], NN)
        x = x_rows[:, :, cols].astype(F32)
        mixed = modf[2:3, cols] * proj
        out_stage[:, :, cols] = (x + mixed.reshape(x.shape)).astype(BF)
    wait_recv(cz_c[0])
    wait_recv(cz_c[1])
    oz_c = [from_frames(out_stage, out_mid[i], ozs, ozr, i, cols) for i, cols in enumerate(parts)]
    o1_c = group_copies(o1_send, o1_recv, o1s, o1r)
    o2_c = group_copies(o2_send, o2_recv, o2s, o2r)
    start(oz_c[0])
    start(oz_c[1])

    whole_part = slice(None)

    def output_on(i):
        wait_recv(oz_c[i])
        spread_frames(out_mid[i], starts[3], o1_send[i], whole_part)
        start(o1_c[i])

    def gated_step(r, carry):
        normed_rows = pl.ds(r * rows, rows)
        att[normed_rows, :] = (ct_rows[r].astype(F32) * modf[2:3, :]).astype(BF)
        return carry

    lax.fori_loop(0, frames, gated_step, 0)

    for cols in col_tiles:
        qkv[:, cols] = dot(att[...], wout[cols, :], NT).astype(BF)
    for h in range(HEADS):
        dop[:, h * LANES : (h + 1) * LANES] = padded(qkv, h * head)

    segments = part_send.shape[0]
    per = HEADS // segments

    def back_begin(h):
        do = dop[:, spot_of(h)] * inverse[h]
        total = jnp.sum((do * op[:, spot_of(h)]).T, axis=0, keepdims=True)
        do = do.astype(BF)
        return do, total, dot(head_keys(vp, h), do, NT)

    def back_end(h, seg, j, do, total, dp):
        spot = spot_of(h)
        p = probs[h]
        ds = (p * (dp - total)).astype(BF)
        dv = dot(p, do, NN)
        dk = dot(ds, qp[:, spot], NN) * factor
        op[:, spot] = (dot(head_keys(kp, h), ds, TN) * factor).T.astype(BF)
        dk_own[:, spot] = dk[:half]
        dv_own[:, spot] = dv[:half]
        part_send[seg, 0, :, spot_of(j)] = dk[half:].astype(BF)
        part_send[seg, 1, :, spot_of(j)] = dv[half:].astype(BF)

    part_c = []
    for seg in range(segments):
        begun = back_begin(seg * per)
        for j in range(per):
            h = seg * per + j
            upcoming = back_begin(h + 1) if j + 1 < per else None
            back_end(h, seg, j, *begun)
            begun = upcoming
        copy = remote(part_send.at[seg], part_recv.at[seg], ps.at[seg], pr.at[seg], other)
        copy.start()
        part_c.append(copy)
    output_on(0)
    for h in range(HEADS):
        qkv[:, h * head : (h + 1) * head] = op[:, h * LANES : h * LANES + head]
    for seg in range(segments):
        part_c[seg].wait_recv()
        for j in range(per):
            h = seg * per + j
            spot = slice(h * LANES, (h + 1) * LANES)
            there = slice(j * LANES, (j + 1) * LANES)
            dk = (dk_own[:, spot] + part_recv[seg, 0, :, there].astype(F32)).astype(BF)
            dv = (dv_own[:, spot] + part_recv[seg, 1, :, there].astype(F32)).astype(BF)
            qkv[:, width + h * head : width + (h + 1) * head] = dk[:, :head]
            qkv[:, 2 * width + h * head : 2 * width + (h + 1) * head] = dv[:, :head]

    for cols in col_tiles:
        att[:, cols] = dot(qkv[:, : 3 * width], wqkv[cols, :], NT).astype(BF)

    output_on(1)

    gz_c = from_frames(grad_stage, grad_ref, gs, gr, 0, whole)
    for r in range(zs):
        _, xhat, inv = norm_parts(r)
        dhat = att[r * rows : (r + 1) * rows, :].astype(F32) * (1.0 + modf[1:2, :])
        m1 = jnp.mean(dhat, axis=-1, keepdims=True)
        m2 = jnp.mean(dhat * xhat, axis=-1, keepdims=True)
        grad_stage[r] = (ct_rows[r].astype(F32) + inv * (dhat - m1 - xhat * m2)).astype(BF)
        gz_c[r].start()

    for i in range(2):
        wait_recv(o1_c[i])
        pass_on(o1_recv[i], starts[4], o2_send[i])
        start(o2_c[i])
    for i, cols in enumerate(parts):
        wait_recv(o2_c[i])
        join_frames(o2_recv[i], starts[5], out_ref, cols)
    wait_recv(gz_c)

    for copies in [x_c, mod_c, gz_c] + c1_c + c2_c + cz_c + oz_c + o1_c + o2_c:
        wait_send(copies)
    k_c.wait_send()
    v_c.wait_send()
    for copy in part_c:
        copy.wait_send()


def place(out_from, grad_from, out_ref, grad_ref, held, in_sem, out_sem):
    arrays = [(out_from, out_ref), (grad_from, grad_ref)]
    spots = [(n, i) for i in range(out_ref.shape[0]) for n in range(2)]
    come = [pltpu.make_async_copy(arrays[n][0].at[i], held.at[n, i], in_sem.at[n, i]) for n, i in spots]
    go = [pltpu.make_async_copy(held.at[n, i], arrays[n][1].at[i], out_sem.at[n, i]) for n, i in spots]
    for copy in come:
        copy.start()
    for before, after in zip(come, go):
        before.wait()
        after.start()
    for copy in go:
        copy.wait()


def local(latents, route, counts, modulation, w_qkv, w_out, cotangent):
    frames, rows, width = latents.shape
    groups = lax.axis_size("grp")
    half = frames * rows
    padded = HEADS * LANES
    segments = 2
    piece = (frames, rows, width)
    middle = -(-width // LANES // 2) * LANES
    widths = (middle, width - middle)
    dma = pltpu.SemaphoreType.DMA
    vmem = pltpu.VMEM
    block = jax.ShapeDtypeStruct(piece, BF)
    scratch = [vmem(w_qkv.shape, BF), vmem(w_out.shape, BF), vmem(piece, BF)]
    scratch += [tuple(vmem((groups, rows // 2, some), BF) for some in widths)] * 8
    scratch += [vmem(piece, BF)] * 3 + [tuple(vmem((frames, rows, some), BF) for some in widths), vmem(piece, BF)]
    scratch += [vmem((groups, 3, width), F32)] * 2
    scratch += [
        vmem((8, width), F32),
        vmem(piece, BF),
        vmem((half, width), BF),
        vmem((half, 3 * width + LANES), BF),
        vmem((half, padded), BF),
        vmem((2, half, padded), BF),
        vmem((2, half, padded), BF),
        vmem((HEADS, 2 * half, half), BF),
        vmem((half, padded), BF),
        vmem((half, width), BF),
        vmem((half, padded), BF),
        vmem((HEADS, half, LANES), F32),
        vmem((half, padded), F32),
        vmem((half, padded), F32),
        vmem((segments, 2, half, padded // segments), BF),
        vmem((segments, 2, half, padded // segments), BF),
        vmem((1, LANES), jnp.int32),
        pltpu.SMEM((1, LANES), jnp.int32),
        dma((4,)),
    ]
    along_z, across = dma((2, frames)), dma((2, groups))
    scratch += [along_z] * 2 + [dma((groups,))] * 2 + [across] * 4 + [along_z] * 2 + [dma((2,))] * 2
    scratch += [along_z] * 2 + [across] * 4 + [dma((segments,))] * 2 + [along_z] * 2
    in_vmem = pl.BlockSpec(memory_space=vmem)
    in_smem = pl.BlockSpec(memory_space=pltpu.SMEM)
    anywhere = pl.BlockSpec(memory_space=pl.ANY)
    results = pl.pallas_call(
        functools.partial(kernel, groups),
        out_shape=(block, block),
        in_specs=[in_smem, in_smem, in_vmem, anywhere, anywhere, in_vmem, anywhere, anywhere],
        out_specs=(in_vmem, in_vmem),
        scratch_shapes=scratch,
        compiler_params=pltpu.CompilerParams(
            collective_id=0, has_side_effects=True, vmem_limit_bytes=60 * 1024 * 1024
        ),
    )(route, counts, route.reshape(1, -1), latents, cotangent, modulation.transpose(1, 0, 2), w_qkv, w_out)
    return pl.pallas_call(
        place,
        out_shape=(block, block),
        in_specs=[anywhere, anywhere],
        out_specs=(anywhere, anywhere),
        scratch_shapes=[vmem((2,) + piece, BF), dma((2, frames)), dma((2, frames))],
        compiler_params=pltpu.CompilerParams(vmem_limit_bytes=60 * 1024 * 1024),
    )(*results)


def solution(mesh):
    rows = P("grp", "sp", None)
    return jax.shard_map(
        local,
        mesh=mesh,
        in_specs=(rows, P(), P("grp", None), P("grp", None, None), P(), P(), rows),
        out_specs=(rows, rows),
        check_vma=False,
    )
```

```python
import functools
import math

import jax
import jax.numpy as jnp
from jax import lax
from jax.experimental import pallas as pl
from jax.experimental.pallas import tpu as pltpu
from jax.sharding import PartitionSpec as P

MESH = pl.DeviceIdType.MESH
HEADS = 16
LANES = 128
EPS = 1e-06
NT = (((1,), (1,)), ((), ()))
NN = (((1,), (0,)), ((), ()))
TN = (((0,), (0,)), ((), ()))
BF = jnp.bfloat16
F32 = jnp.float32


def dot(a, b, dims):
    return lax.dot_general(a, b, dims, preferred_element_type=F32)


def bits_of(number):
    return number.bit_length() - 1


def colour(route_row, groups, frames):
    edges = groups * frames
    shift = bits_of(frames)
    square = (edges, edges)
    r_wide = jnp.broadcast_to(route_row.astype(F32), square)
    r_row, r_col = r_wide.astype(jnp.int32), r_wide.T.astype(jnp.int32)
    k_row = lax.broadcasted_iota(jnp.int32, square, 1)
    k_col = lax.broadcasted_iota(jnp.int32, square, 0)
    same_source = (k_row >> shift) == (k_col >> shift)
    same_target = (r_row >> shift) == (r_col >> shift)
    as_bf = lambda flag: jnp.where(flag, 1.0, 0.0).astype(BF)
    eye = jnp.where(k_row == k_col, 1.0, 0.0)
    c_row = jnp.zeros((1, edges), jnp.int32)
    c_col = jnp.zeros((edges, 1), jnp.int32)
    for level in range(shift):
        same = c_row == c_col
        s_pair = as_bf(same & same_source & ((k_row >> level) == ((k_col >> level) ^ 1)))
        t_pair = as_bf(same & same_target & ((r_row >> level) == ((r_col >> level) ^ 1)))
        reach = (dot(s_pair, t_pair, NN) + dot(t_pair, s_pair, NN) + eye).astype(BF)
        for _ in range(max(1, bits_of(edges) - 2 - level)):
            reach = dot(reach, reach, NN).astype(BF)
        mine = reach > 0
        partner = dot(s_pair, reach, NN) > 0
        first = lambda flag, ids, axis: jnp.min(jnp.where(flag, ids, edges), axis=axis, keepdims=True)
        bit_row = (first(mine, k_col, 0) < first(partner, k_col, 0)).astype(jnp.int32)
        bit_col = (first(mine, k_row, 1) < first(partner, k_row, 1)).astype(jnp.int32)
        c_row = c_row * 2 + bit_row
        c_col = c_col * 2 + bit_col
    return c_col, r_col[:, :1], k_col[:, :1]


def table_starts(groups, frames):
    starts = [0]
    for length in (frames, groups, frames, frames, groups, frames):
        starts.append(starts[-1] + length)
    return starts


def make_table(route_row, groups, frames, me):
    c, r, k = colour(route_row, groups, frames)
    shift = bits_of(frames)
    starts = table_starts(groups, frames)
    t = lax.broadcasted_iota(jnp.int32, (1, LANES), 1)
    source, target = k >> shift, r >> shift
    by_source, by_target = source * frames + c, target * frames + c
    via = me // 2
    runs = [
        (by_target, me * frames + t - starts[0], r & (frames - 1)),
        (by_source, (t - starts[1]) * frames + via, target),
        (k, me * frames + t - starts[2], c),
        (by_source, me * frames + t - starts[3], k & (frames - 1)),
        (by_target, (t - starts[4]) * frames + via, source),
        (r, me * frames + t - starts[5], c),
    ]
    table = jnp.zeros((1, LANES), jnp.int32)
    for i, (key, wanted, value) in enumerate(runs):
        found = jnp.sum(jnp.where(key == wanted, value, 0), axis=0, keepdims=True)
        found = jnp.clip(found, 0, starts[i + 1] - starts[i] - 1)
        table = jnp.where((t >= starts[i]) & (t < starts[i + 1]), found, table)
    return table


def kernel(
    groups,
    route,
    counts,
    route_row,
    lat,
    ct_hbm,
    mod,
    wqkv_hbm,
    wout_hbm,
    out_ref,
    grad_ref,
    wqkv,
    wout,
    ct,
    c1_send,
    c1_recv,
    c2_send,
    c2_recv,
    o1_send,
    o1_recv,
    o2_send,
    o2_recv,
    ct_stage,
    ct_rows,
    out_stage,
    out_mid,
    grad_stage,
    mod_send,
    mod_recv,
    modf,
    x_rows,
    normed,
    qkv,
    qp,
    kp,
    vp,
    probs,
    op,
    att,
    dop,
    inverse,
    dk_own,
    dv_own,
    part_send,
    part_recv,
    tab_row,
    tab,
    w_sem,
    xs,
    xr,
    ms,
    mr,
    c1s,
    c1r,
    c2s,
    c2r,
    czs,
    czr,
    kvs,
    kvr,
    ozs,
    ozr,
    o1s,
    o1r,
    o2s,
    o2r,
    ps,
    pr,
    gs,
    gr,
):
    frames, rows, width = ct_hbm.shape
    head = width // HEADS
    zs = frames
    half = frames * rows
    me = lax.axis_index("grp")
    sp = lax.axis_index("sp")
    z = sp // 2
    core = sp % 2
    starts = table_starts(groups, frames)
    piece = rows // 2

    def z_dev(d):
        return {"sp": lax.rem(z + d, zs) * 2 + core}

    def g_dev(d):
        return {"grp": lax.rem(me + d, groups)}

    other = {"sp": z * 2 + (1 - core)}

    w1 = pltpu.make_async_copy(wqkv_hbm, wqkv, w_sem.at[0])
    w2 = pltpu.make_async_copy(wout_hbm, wout, w_sem.at[1])
    barrier = pltpu.get_barrier_semaphore()
    for d in range(1, zs):
        pl.semaphore_signal(barrier, inc=1, device_id=z_dev(d), device_id_type=MESH)
    for d in range(1, groups):
        pl.semaphore_signal(barrier, inc=1, device_id=g_dev(d), device_id_type=MESH)
    pl.semaphore_signal(barrier, inc=1, device_id=other, device_id_type=MESH)
    ct_c = pltpu.make_async_copy(ct_hbm, ct, w_sem.at[3])
    ct_c.start()
    w1.start()
    w2.start()

    def remote(src, dst, s_sem, r_sem, dev):
        return pltpu.make_async_remote_copy(
            src_ref=src, dst_ref=dst, send_sem=s_sem, recv_sem=r_sem, device_id=dev, device_id_type=MESH
        )

    middle = -(-width // LANES // 2) * LANES
    parts = [pl.ds(0, middle), pl.ds(middle, width - middle)]

    def group_copies(src, dst, s_sem, r_sem):
        def copies(i):
            own = pltpu.make_async_copy(src[i].at[me], dst[i].at[me], s_sem.at[i, 0])
            return [own] + [
                remote(src[i].at[lax.rem(me + d, groups)], dst[i].at[me], s_sem.at[i, d], r_sem.at[i, d], g_dev(d))
                for d in range(1, groups)
            ]

        return [copies(i) for i in range(2)]

    def mod_copies():
        own = pltpu.make_async_copy(mod_send.at[me], mod_recv.at[me], ms.at[0])
        return [own] + [
            remote(mod_send.at[lax.rem(me + d, groups)], mod_recv.at[me], ms.at[d], mr.at[d], g_dev(d))
            for d in range(1, groups)
        ]

    near_first = sorted(range(1, zs), key=lambda d: min(d, zs - d))

    ahead = [0] + [zs - d for d in near_first]

    def to_frames(src, dst, s_sem, r_sem, i, cols):
        own = pltpu.make_async_copy(src.at[z, :, cols], dst.at[0, :, cols], s_sem.at[i, 0])
        return [own] + [
            remote(
                src.at[lax.rem(z + d, zs), :, cols],
                dst.at[n + 1, :, cols],
                s_sem.at[i, d],
                r_sem.at[i, d],
                z_dev(d),
            )
            for n, d in enumerate(near_first)
        ]

    def from_frames(src, dst, s_sem, r_sem, i, cols):
        own = pltpu.make_async_copy(src.at[0, :, cols], dst.at[z], s_sem.at[i, 0])
        return [own] + [
            remote(src.at[n, :, cols], dst.at[z], s_sem.at[i, d], r_sem.at[i, d], z_dev(d))
            for n, d in list(enumerate(ahead))[1:]
        ]

    def start(copies):
        for copy in copies:
            copy.start()

    def wait_recv(copies):
        copies[0].wait()
        for copy in copies[1:]:
            copy.wait_recv()

    def wait_send(copies):
        for copy in copies[1:]:
            copy.wait_send()

    whole = pl.ds(0, width)
    tab_row[...] = make_table(route_row[...], groups, frames, me)
    tab_c = pltpu.make_async_copy(tab_row, tab, w_sem.at[2])
    tab_c.start()

    ends = [counts[0, 0]]
    for i in range(1, counts.shape[1] - 1):
        ends.append(ends[-1] + counts[0, i])
    for g in range(groups):
        slot = lax.rem(route[g * frames + z], frames)
        clip = sum([jnp.where(slot >= end, 1, 0) for end in ends])
        for i in range(3):
            mod_send[g, i : i + 1, :] = mod[i, pl.ds(clip, 1), :]

    tab_c.wait()
    ct_c.wait()

    def spread_frames(source, first, send, cols):
        for m in range(groups):
            send[m] = source[tab[0, first + m // 2], (m % 2) * piece : (m % 2 + 1) * piece, cols]

    def pass_on(received, first, send):
        for g in range(groups):
            send[g] = received[tab[0, first + g]]

    def join_frames(received, first, target, cols):
        for f in range(frames):
            c = tab[0, first + f]
            target[f, :piece, cols] = received[2 * c]
            target[f, piece:, cols] = received[2 * c + 1]

    for i, cols in enumerate(parts):
        spread_frames(ct, starts[0], c1_send[i], cols)
    pl.semaphore_wait(barrier, zs - 1 + groups - 1 + 1)

    x_c = to_frames(lat, x_rows, xs, xr, 0, whole)
    start(x_c)
    c1_c = group_copies(c1_send, c1_recv, c1s, c1r)
    c2_c = group_copies(c2_send, c2_recv, c2s, c2r)
    cz_c = [to_frames(ct_stage, ct_rows, czs, czr, i, cols) for i, cols in enumerate(parts)]
    mod_c = mod_copies()
    start(c1_c[0])
    start(c1_c[1])
    start(mod_c)

    def cotangent_on(i):
        wait_recv(c2_c[i])
        join_frames(c2_recv[i], starts[2], ct_stage, parts[i])
        start(cz_c[i])

    qkv[:, 3 * width :] = jnp.zeros((half, qkv.shape[1] - 3 * width), BF)
    for i in range(2):
        wait_recv(c1_c[i])
        pass_on(c1_recv[i], starts[1], c2_send[i])
        start(c2_c[i])
    wait_recv(mod_c)
    modf[:3, :] = mod_recv[route[me * frames + z] // frames]

    def norm_parts(r):
        x = x_rows[r].astype(F32)
        center = jnp.mean(x, axis=-1, keepdims=True)
        spread = x - center
        inv = lax.rsqrt(jnp.mean(spread * spread, axis=-1, keepdims=True) + EPS)
        return x, spread * inv, inv

    lane = lax.broadcasted_iota(jnp.int32, (half, LANES), 1)

    def arrive(first, last):
        for r in range(first, last):
            x_c[r].wait() if r == 0 else x_c[r].wait_recv()
            _, xhat, _ = norm_parts(r)
            normed[r * rows : (r + 1) * rows, :] = (xhat * (1.0 + modf[1:2, :]) + modf[0:1, :]).astype(BF)

    def project(start_col, stop_col, some):
        for at in range(start_col, stop_col, 256):
            cols = slice(at, min(at + 256, stop_col))
            qkv[some, cols] = dot(normed[some, :], wqkv[:, cols], NN).astype(BF)

    def padded(source, start_col):
        piece = source[:, start_col : start_col + LANES]
        return jnp.where(lane < head, piece, jnp.zeros_like(piece))

    k_c = remote(kp.at[0], kp.at[1], kvs.at[0], kvr.at[0], other)
    v_c = remote(vp.at[0], vp.at[1], kvs.at[1], kvr.at[1], other)
    k_stop = width + -(-width // 256) * 256
    arrive(0, zs // 2)
    w1.wait()
    early, late = slice(0, half // 2), slice(half // 2, half)
    project(width, 3 * width, early)
    project(0, width, early)
    cotangent_on(0)
    arrive(zs // 2, zs)
    project(width, k_stop, late)
    for h in range(HEADS):
        kp[0, :, h * LANES : (h + 1) * LANES] = padded(qkv, width + h * head)
    k_c.start()
    cotangent_on(1)
    project(k_stop, 3 * width, late)
    for h in range(HEADS):
        piece_v = padded(qkv, 2 * width + h * head)
        vp[0, :, h * LANES : (h + 1) * LANES] = jnp.where(lane == head, jnp.ones_like(piece_v), piece_v)
    v_c.start()
    project(0, width, late)
    for h in range(HEADS):
        qp[:, h * LANES : (h + 1) * LANES] = padded(qkv, h * head)
    k_c.wait_recv()
    v_c.wait_recv()

    factor = head**-0.5
    log2 = factor * math.log2(math.e)
    def spot_of(h):
        return pl.ds(h * LANES, LANES)

    def head_keys(ref, h):
        return ref[:, :, spot_of(h)].reshape(2 * half, LANES)

    def scores_of(h):
        return dot(head_keys(kp, h), qp[:, spot_of(h)], NT)

    def attend(h, scores):
        top = jnp.max(scores, axis=0, keepdims=True)
        ex = jnp.exp2((scores - top) * log2).astype(BF)
        probs[h] = ex
        mixed = dot(head_keys(vp, h), ex, TN).T
        inv = 1.0 / mixed[:, head : head + 1]
        inverse[h] = jnp.broadcast_to(inv, (half, LANES))
        op[:, spot_of(h)] = (mixed * inv).astype(BF)

    scores = scores_of(0)
    for h in range(HEADS):
        upcoming = scores_of(h + 1) if h + 1 < HEADS else None
        attend(h, scores)
        scores = upcoming

    for h in range(HEADS):
        att[:, h * head : (h + 1) * head] = op[:, h * LANES : h * LANES + head]

    w2.wait()

    col_tiles = [slice(at, min(at + 256, width)) for at in range(0, width, 256)]
    for cols in col_tiles:
        proj = dot(att[...], wout[:, cols], NN)
        x = x_rows[:, :, cols].astype(F32)
        mixed = modf[2:3, cols] * proj
        out_stage[:, :, cols] = (x + mixed.reshape(x.shape)).astype(BF)
    wait_recv(cz_c[0])
    wait_recv(cz_c[1])
    oz_c = [from_frames(out_stage, out_mid[i], ozs, ozr, i, cols) for i, cols in enumerate(parts)]
    o1_c = group_copies(o1_send, o1_recv, o1s, o1r)
    o2_c = group_copies(o2_send, o2_recv, o2s, o2r)
    start(oz_c[0])

    whole_part = slice(None)

    def output_on(i):
        wait_recv(oz_c[i])
        spread_frames(out_mid[i], starts[3], o1_send[i], whole_part)
        start(o1_c[i])

    def gated_step(r, carry):
        normed_rows = pl.ds(r * rows, rows)
        att[normed_rows, :] = (ct_rows[r].astype(F32) * modf[2:3, :]).astype(BF)
        return carry

    lax.fori_loop(0, frames, gated_step, 0)

    for cols in col_tiles:
        qkv[:, cols] = dot(att[...], wout[cols, :], NT).astype(BF)
    for h in range(HEADS):
        dop[:, h * LANES : (h + 1) * LANES] = padded(qkv, h * head)

    start(oz_c[1])
    segments = part_send.shape[0]
    per = HEADS // segments

    def back_begin(h):
        do = dop[:, spot_of(h)] * inverse[h]
        total = jnp.sum((do * op[:, spot_of(h)]).T, axis=0, keepdims=True)
        do = do.astype(BF)
        return do, total, dot(head_keys(vp, h), do, NT)

    def back_end(h, seg, j, do, total, dp):
        spot = spot_of(h)
        p = probs[h]
        ds = (p * (dp - total)).astype(BF)
        dv = dot(p, do, NN)
        dk = dot(ds, qp[:, spot], NN) * factor
        op[:, spot] = (dot(head_keys(kp, h), ds, TN) * factor).T.astype(BF)
        dk_own[:, spot] = dk[:half]
        dv_own[:, spot] = dv[:half]
        part_send[seg, 0, :, spot_of(j)] = dk[half:].astype(BF)
        part_send[seg, 1, :, spot_of(j)] = dv[half:].astype(BF)

    part_c = []
    for seg in range(segments):
        begun = back_begin(seg * per)
        for j in range(per):
            h = seg * per + j
            upcoming = back_begin(h + 1) if j + 1 < per else None
            back_end(h, seg, j, *begun)
            begun = upcoming
        copy = remote(part_send.at[seg], part_recv.at[seg], ps.at[seg], pr.at[seg], other)
        copy.start()
        part_c.append(copy)
    output_on(0)
    for h in range(HEADS):
        qkv[:, h * head : (h + 1) * head] = op[:, h * LANES : h * LANES + head]
    for seg in range(segments):
        part_c[seg].wait_recv()
        for j in range(per):
            h = seg * per + j
            spot = slice(h * LANES, (h + 1) * LANES)
            there = slice(j * LANES, (j + 1) * LANES)
            dk = (dk_own[:, spot] + part_recv[seg, 0, :, there].astype(F32)).astype(BF)
            dv = (dv_own[:, spot] + part_recv[seg, 1, :, there].astype(F32)).astype(BF)
            qkv[:, width + h * head : width + (h + 1) * head] = dk[:, :head]
            qkv[:, 2 * width + h * head : 2 * width + (h + 1) * head] = dv[:, :head]

    for cols in col_tiles:
        att[:, cols] = dot(qkv[:, : 3 * width], wqkv[cols, :], NT).astype(BF)

    output_on(1)

    gz_c = from_frames(grad_stage, grad_ref, gs, gr, 0, whole)
    for r in range(zs):
        _, xhat, inv = norm_parts(r)
        dhat = att[r * rows : (r + 1) * rows, :].astype(F32) * (1.0 + modf[1:2, :])
        m1 = jnp.mean(dhat, axis=-1, keepdims=True)
        m2 = jnp.mean(dhat * xhat, axis=-1, keepdims=True)
        grad_stage[r] = (ct_rows[r].astype(F32) + inv * (dhat - m1 - xhat * m2)).astype(BF)
        gz_c[r].start()

    for i in range(2):
        wait_recv(o1_c[i])
        pass_on(o1_recv[i], starts[4], o2_send[i])
        start(o2_c[i])
    for i, cols in enumerate(parts):
        wait_recv(o2_c[i])
        join_frames(o2_recv[i], starts[5], out_ref, cols)
    wait_recv(gz_c)

    for copies in [x_c, mod_c, gz_c] + c1_c + c2_c + cz_c + oz_c + o1_c + o2_c:
        wait_send(copies)
    k_c.wait_send()
    v_c.wait_send()
    for copy in part_c:
        copy.wait_send()


def place(out_from, grad_from, out_ref, grad_ref, held, in_sem, out_sem):
    arrays = [(out_from, out_ref), (grad_from, grad_ref)]
    spots = [(n, i) for i in range(out_ref.shape[0]) for n in range(2)]
    come = [pltpu.make_async_copy(arrays[n][0].at[i], held.at[n, i], in_sem.at[n, i]) for n, i in spots]
    go = [pltpu.make_async_copy(held.at[n, i], arrays[n][1].at[i], out_sem.at[n, i]) for n, i in spots]
    for copy in come:
        copy.start()
    for before, after in zip(come, go):
        before.wait()
        after.start()
    for copy in go:
        copy.wait()


def local(latents, route, counts, modulation, w_qkv, w_out, cotangent):
    frames, rows, width = latents.shape
    groups = lax.axis_size("grp")
    half = frames * rows
    padded = HEADS * LANES
    segments = 2
    piece = (frames, rows, width)
    middle = -(-width // LANES // 2) * LANES
    widths = (middle, width - middle)
    dma = pltpu.SemaphoreType.DMA
    vmem = pltpu.VMEM
    block = jax.ShapeDtypeStruct(piece, BF)
    scratch = [vmem(w_qkv.shape, BF), vmem(w_out.shape, BF), vmem(piece, BF)]
    scratch += [tuple(vmem((groups, rows // 2, some), BF) for some in widths)] * 8
    scratch += [vmem(piece, BF)] * 3 + [tuple(vmem((frames, rows, some), BF) for some in widths), vmem(piece, BF)]
    scratch += [vmem((groups, 3, width), F32)] * 2
    scratch += [
        vmem((8, width), F32),
        vmem(piece, BF),
        vmem((half, width), BF),
        vmem((half, 3 * width + LANES), BF),
        vmem((half, padded), BF),
        vmem((2, half, padded), BF),
        vmem((2, half, padded), BF),
        vmem((HEADS, 2 * half, half), BF),
        vmem((half, padded), BF),
        vmem((half, width), BF),
        vmem((half, padded), BF),
        vmem((HEADS, half, LANES), F32),
        vmem((half, padded), F32),
        vmem((half, padded), F32),
        vmem((segments, 2, half, padded // segments), BF),
        vmem((segments, 2, half, padded // segments), BF),
        vmem((1, LANES), jnp.int32),
        pltpu.SMEM((1, LANES), jnp.int32),
        dma((4,)),
    ]
    along_z, across = dma((2, frames)), dma((2, groups))
    scratch += [along_z] * 2 + [dma((groups,))] * 2 + [across] * 4 + [along_z] * 2 + [dma((2,))] * 2
    scratch += [along_z] * 2 + [across] * 4 + [dma((segments,))] * 2 + [along_z] * 2
    in_vmem = pl.BlockSpec(memory_space=vmem)
    in_smem = pl.BlockSpec(memory_space=pltpu.SMEM)
    anywhere = pl.BlockSpec(memory_space=pl.ANY)
    results = pl.pallas_call(
        functools.partial(kernel, groups),
        out_shape=(block, block),
        in_specs=[in_smem, in_smem, in_vmem, anywhere, anywhere, in_vmem, anywhere, anywhere],
        out_specs=(in_vmem, in_vmem),
        scratch_shapes=scratch,
        compiler_params=pltpu.CompilerParams(
            collective_id=0, has_side_effects=True, vmem_limit_bytes=60 * 1024 * 1024
        ),
    )(route, counts, route.reshape(1, -1), latents, cotangent, modulation.transpose(1, 0, 2), w_qkv, w_out)
    return pl.pallas_call(
        place,
        out_shape=(block, block),
        in_specs=[anywhere, anywhere],
        out_specs=(anywhere, anywhere),
        scratch_shapes=[vmem((2,) + piece, BF), dma((2, frames)), dma((2, frames))],
        compiler_params=pltpu.CompilerParams(vmem_limit_bytes=60 * 1024 * 1024),
    )(*results)


def solution(mesh):
    rows = P("grp", "sp", None)
    return jax.shard_map(
        local,
        mesh=mesh,
        in_specs=(rows, P(), P("grp", None), P("grp", None, None), P(), P(), rows),
        out_specs=(rows, rows),
        check_vma=False,
    )
```

```python
import functools
import math

import jax
import jax.numpy as jnp
from jax import lax
from jax.experimental import pallas as pl
from jax.experimental.pallas import tpu as pltpu
from jax.sharding import PartitionSpec as P

MESH = pl.DeviceIdType.MESH
HEADS = 16
LANES = 128
EPS = 1e-06
NT = (((1,), (1,)), ((), ()))
NN = (((1,), (0,)), ((), ()))
TN = (((0,), (0,)), ((), ()))
BF = jnp.bfloat16
F32 = jnp.float32


def dot(a, b, dims):
    return lax.dot_general(a, b, dims, preferred_element_type=F32)


def bits_of(number):
    return number.bit_length() - 1


def colour(route_row, groups, frames):
    edges = groups * frames
    shift = bits_of(frames)
    square = (edges, edges)
    r_wide = jnp.broadcast_to(route_row.astype(F32), square)
    r_row, r_col = r_wide.astype(jnp.int32), r_wide.T.astype(jnp.int32)
    k_row = lax.broadcasted_iota(jnp.int32, square, 1)
    k_col = lax.broadcasted_iota(jnp.int32, square, 0)
    same_source = (k_row >> shift) == (k_col >> shift)
    same_target = (r_row >> shift) == (r_col >> shift)
    as_bf = lambda flag: jnp.where(flag, 1.0, 0.0).astype(BF)
    eye = jnp.where(k_row == k_col, 1.0, 0.0)
    c_row = jnp.zeros((1, edges), jnp.int32)
    c_col = jnp.zeros((edges, 1), jnp.int32)
    for level in range(shift):
        same = c_row == c_col
        s_pair = as_bf(same & same_source & ((k_row >> level) == ((k_col >> level) ^ 1)))
        t_pair = as_bf(same & same_target & ((r_row >> level) == ((r_col >> level) ^ 1)))
        reach = (dot(s_pair, t_pair, NN) + dot(t_pair, s_pair, NN) + eye).astype(BF)
        for _ in range(max(1, bits_of(edges) - 2 - level)):
            reach = dot(reach, reach, NN).astype(BF)
        mine = reach > 0
        partner = dot(s_pair, reach, NN) > 0
        first = lambda flag, ids, axis: jnp.min(jnp.where(flag, ids, edges), axis=axis, keepdims=True)
        bit_row = (first(mine, k_col, 0) < first(partner, k_col, 0)).astype(jnp.int32)
        bit_col = (first(mine, k_row, 1) < first(partner, k_row, 1)).astype(jnp.int32)
        c_row = c_row * 2 + bit_row
        c_col = c_col * 2 + bit_col
    return c_col, r_col[:, :1], k_col[:, :1]


def table_starts(groups, frames):
    starts = [0]
    for length in (frames, groups, frames, frames, groups, frames):
        starts.append(starts[-1] + length)
    return starts


def make_table(route_row, groups, frames, me):
    c, r, k = colour(route_row, groups, frames)
    shift = bits_of(frames)
    starts = table_starts(groups, frames)
    t = lax.broadcasted_iota(jnp.int32, (1, LANES), 1)
    source, target = k >> shift, r >> shift
    by_source, by_target = source * frames + c, target * frames + c
    via = me // 2
    runs = [
        (by_target, me * frames + t - starts[0], r & (frames - 1)),
        (by_source, (t - starts[1]) * frames + via, target),
        (k, me * frames + t - starts[2], c),
        (by_source, me * frames + t - starts[3], k & (frames - 1)),
        (by_target, (t - starts[4]) * frames + via, source),
        (r, me * frames + t - starts[5], c),
    ]
    table = jnp.zeros((1, LANES), jnp.int32)
    for i, (key, wanted, value) in enumerate(runs):
        found = jnp.sum(jnp.where(key == wanted, value, 0), axis=0, keepdims=True)
        found = jnp.clip(found, 0, starts[i + 1] - starts[i] - 1)
        table = jnp.where((t >= starts[i]) & (t < starts[i + 1]), found, table)
    return table


def kernel(
    groups,
    route,
    counts,
    route_row,
    lat,
    ct_hbm,
    mod,
    wqkv_hbm,
    wout_hbm,
    out_ref,
    grad_ref,
    wqkv,
    wout,
    ct,
    c1_send,
    c1_recv,
    c2_send,
    c2_recv,
    o1_send,
    o1_recv,
    o2_send,
    o2_recv,
    ct_stage,
    ct_rows,
    out_stage,
    out_mid,
    grad_stage,
    mod_send,
    mod_recv,
    modf,
    x_rows,
    normed,
    qkv,
    qp,
    kp,
    vp,
    probs,
    op,
    att,
    dop,
    inverse,
    dk_own,
    dv_own,
    part_send,
    part_recv,
    tab_row,
    tab,
    w_sem,
    xs,
    xr,
    ms,
    mr,
    c1s,
    c1r,
    c2s,
    c2r,
    czs,
    czr,
    kvs,
    kvr,
    ozs,
    ozr,
    o1s,
    o1r,
    o2s,
    o2r,
    ps,
    pr,
    gs,
    gr,
):
    frames, rows, width = ct_hbm.shape
    head = width // HEADS
    zs = frames
    half = frames * rows
    me = lax.axis_index("grp")
    sp = lax.axis_index("sp")
    z = sp // 2
    core = sp % 2
    starts = table_starts(groups, frames)
    piece = rows // 2

    def z_dev(d):
        return {"sp": lax.rem(z + d, zs) * 2 + core}

    def g_dev(d):
        return {"grp": lax.rem(me + d, groups)}

    other = {"sp": z * 2 + (1 - core)}

    w1 = pltpu.make_async_copy(wqkv_hbm, wqkv, w_sem.at[0])
    w2 = pltpu.make_async_copy(wout_hbm, wout, w_sem.at[1])
    barrier = pltpu.get_barrier_semaphore()
    for d in range(1, zs):
        pl.semaphore_signal(barrier, inc=1, device_id=z_dev(d), device_id_type=MESH)
    for d in range(1, groups):
        pl.semaphore_signal(barrier, inc=1, device_id=g_dev(d), device_id_type=MESH)
    pl.semaphore_signal(barrier, inc=1, device_id=other, device_id_type=MESH)
    ct_c = pltpu.make_async_copy(ct_hbm, ct, w_sem.at[3])
    ct_c.start()
    w1.start()
    w2.start()

    def remote(src, dst, s_sem, r_sem, dev):
        return pltpu.make_async_remote_copy(
            src_ref=src, dst_ref=dst, send_sem=s_sem, recv_sem=r_sem, device_id=dev, device_id_type=MESH
        )

    middle = -(-width // LANES // 2) * LANES
    parts = [pl.ds(0, middle), pl.ds(middle, width - middle)]

    def group_copies(src, dst, s_sem, r_sem):
        def copies(i):
            own = pltpu.make_async_copy(src[i].at[me], dst[i].at[me], s_sem.at[i, 0])
            return [own] + [
                remote(src[i].at[lax.rem(me + d, groups)], dst[i].at[me], s_sem.at[i, d], r_sem.at[i, d], g_dev(d))
                for d in range(1, groups)
            ]

        return [copies(i) for i in range(2)]

    def mod_copies():
        own = pltpu.make_async_copy(mod_send.at[me], mod_recv.at[me], ms.at[0])
        return [own] + [
            remote(mod_send.at[lax.rem(me + d, groups)], mod_recv.at[me], ms.at[d], mr.at[d], g_dev(d))
            for d in range(1, groups)
        ]

    near_first = sorted(range(1, zs), key=lambda d: min(d, zs - d))

    ahead = [0] + [zs - d for d in near_first]

    def to_frames(src, dst, s_sem, r_sem, i, cols):
        own = pltpu.make_async_copy(src.at[z, :, cols], dst.at[0, :, cols], s_sem.at[i, 0])
        return [own] + [
            remote(
                src.at[lax.rem(z + d, zs), :, cols],
                dst.at[n + 1, :, cols],
                s_sem.at[i, d],
                r_sem.at[i, d],
                z_dev(d),
            )
            for n, d in enumerate(near_first)
        ]

    def from_frames(src, dst, s_sem, r_sem, i, cols):
        own = pltpu.make_async_copy(src.at[0, :, cols], dst.at[z], s_sem.at[i, 0])
        return [own] + [
            remote(src.at[n, :, cols], dst.at[z], s_sem.at[i, d], r_sem.at[i, d], z_dev(d))
            for n, d in list(enumerate(ahead))[1:]
        ]

    def start(copies):
        for copy in copies:
            copy.start()

    def wait_recv(copies):
        copies[0].wait()
        for copy in copies[1:]:
            copy.wait_recv()

    def wait_send(copies):
        for copy in copies[1:]:
            copy.wait_send()

    whole = pl.ds(0, width)
    tab_row[...] = make_table(route_row[...], groups, frames, me)
    tab_c = pltpu.make_async_copy(tab_row, tab, w_sem.at[2])
    tab_c.start()

    ends = [counts[0, 0]]
    for i in range(1, counts.shape[1] - 1):
        ends.append(ends[-1] + counts[0, i])
    for g in range(groups):
        slot = lax.rem(route[g * frames + z], frames)
        clip = sum([jnp.where(slot >= end, 1, 0) for end in ends])
        for i in range(3):
            mod_send[g, i : i + 1, :] = mod[i, pl.ds(clip, 1), :]

    tab_c.wait()
    ct_c.wait()

    def spread_frames(source, first, send, cols):
        for m in range(groups):
            send[m] = source[tab[0, first + m // 2], (m % 2) * piece : (m % 2 + 1) * piece, cols]

    def pass_on(received, first, send):
        for g in range(groups):
            send[g] = received[tab[0, first + g]]

    def join_frames(received, first, target, cols):
        for f in range(frames):
            c = tab[0, first + f]
            target[f, :piece, cols] = received[2 * c]
            target[f, piece:, cols] = received[2 * c + 1]

    for i, cols in enumerate(parts):
        spread_frames(ct, starts[0], c1_send[i], cols)
    pl.semaphore_wait(barrier, zs - 1 + groups - 1 + 1)

    x_c = to_frames(lat, x_rows, xs, xr, 0, whole)
    start(x_c)
    c1_c = group_copies(c1_send, c1_recv, c1s, c1r)
    c2_c = group_copies(c2_send, c2_recv, c2s, c2r)
    cz_c = [to_frames(ct_stage, ct_rows, czs, czr, i, cols) for i, cols in enumerate(parts)]
    mod_c = mod_copies()
    start(c1_c[0])
    start(c1_c[1])
    start(mod_c)

    def cotangent_on(i):
        wait_recv(c2_c[i])
        join_frames(c2_recv[i], starts[2], ct_stage, parts[i])
        start(cz_c[i])

    qkv[:, 3 * width :] = jnp.zeros((half, qkv.shape[1] - 3 * width), BF)
    for i in range(2):
        wait_recv(c1_c[i])
        pass_on(c1_recv[i], starts[1], c2_send[i])
        start(c2_c[i])
    wait_recv(mod_c)
    modf[:3, :] = mod_recv[route[me * frames + z] // frames]

    def norm_parts(r):
        x = x_rows[r].astype(F32)
        center = jnp.mean(x, axis=-1, keepdims=True)
        spread = x - center
        inv = lax.rsqrt(jnp.mean(spread * spread, axis=-1, keepdims=True) + EPS)
        return x, spread * inv, inv

    lane = lax.broadcasted_iota(jnp.int32, (half, LANES), 1)

    def arrive(first, last):
        for r in range(first, last):
            x_c[r].wait() if r == 0 else x_c[r].wait_recv()
            _, xhat, _ = norm_parts(r)
            normed[r * rows : (r + 1) * rows, :] = (xhat * (1.0 + modf[1:2, :]) + modf[0:1, :]).astype(BF)

    def project(start_col, stop_col, some):
        for at in range(start_col, stop_col, 256):
            cols = slice(at, min(at + 256, stop_col))
            qkv[some, cols] = dot(normed[some, :], wqkv[:, cols], NN).astype(BF)

    def padded(source, start_col):
        piece = source[:, start_col : start_col + LANES]
        return jnp.where(lane < head, piece, jnp.zeros_like(piece))

    k_c = remote(kp.at[0], kp.at[1], kvs.at[0], kvr.at[0], other)
    v_c = remote(vp.at[0], vp.at[1], kvs.at[1], kvr.at[1], other)
    k_stop = width + -(-width // 256) * 256
    arrive(0, zs // 2)
    w1.wait()
    early, late = slice(0, half // 2), slice(half // 2, half)
    project(width, 3 * width, early)
    project(0, width, early)
    cotangent_on(0)
    arrive(zs // 2, zs)
    project(width, k_stop, late)
    for h in range(HEADS):
        kp[0, :, h * LANES : (h + 1) * LANES] = padded(qkv, width + h * head)
    k_c.start()
    cotangent_on(1)
    project(k_stop, 3 * width, late)
    for h in range(HEADS):
        piece_v = padded(qkv, 2 * width + h * head)
        vp[0, :, h * LANES : (h + 1) * LANES] = jnp.where(lane == head, jnp.ones_like(piece_v), piece_v)
    v_c.start()
    project(0, width, late)
    for h in range(HEADS):
        qp[:, h * LANES : (h + 1) * LANES] = padded(qkv, h * head)
    k_c.wait_recv()
    v_c.wait_recv()

    factor = head**-0.5
    log2 = factor * math.log2(math.e)
    def spot_of(h):
        return pl.ds(h * LANES, LANES)

    def head_keys(ref, h):
        return ref[:, :, spot_of(h)].reshape(2 * half, LANES)

    def scores_of(h):
        return dot(head_keys(kp, h), qp[:, spot_of(h)], NT)

    def attend(h, scores):
        top = jnp.max(scores, axis=0, keepdims=True)
        ex = jnp.exp2((scores - top) * log2).astype(BF)
        probs[h] = ex
        mixed = dot(head_keys(vp, h), ex, TN).T
        inv = 1.0 / mixed[:, head : head + 1]
        inverse[h] = jnp.broadcast_to(inv, (half, LANES))
        op[:, spot_of(h)] = (mixed * inv).astype(BF)

    scores = scores_of(0)
    for h in range(HEADS):
        upcoming = scores_of(h + 1) if h + 1 < HEADS else None
        attend(h, scores)
        scores = upcoming

    for h in range(HEADS):
        att[:, h * head : (h + 1) * head] = op[:, h * LANES : h * LANES + head]

    w2.wait()

    col_tiles = [slice(at, min(at + 256, width)) for at in range(0, width, 256)]
    for cols in col_tiles:
        proj = dot(att[...], wout[:, cols], NN)
        x = x_rows[:, :, cols].astype(F32)
        mixed = modf[2:3, cols] * proj
        out_stage[:, :, cols] = (x + mixed.reshape(x.shape)).astype(BF)
    wait_recv(cz_c[0])
    wait_recv(cz_c[1])
    oz_c = [from_frames(out_stage, out_mid[i], ozs, ozr, i, cols) for i, cols in enumerate(parts)]
    o1_c = group_copies(o1_send, o1_recv, o1s, o1r)
    o2_c = group_copies(o2_send, o2_recv, o2s, o2r)
    start(oz_c[0])

    whole_part = slice(None)

    def output_on(i):
        wait_recv(oz_c[i])
        spread_frames(out_mid[i], starts[3], o1_send[i], whole_part)
        start(o1_c[i])

    def gated_step(r, carry):
        normed_rows = pl.ds(r * rows, rows)
        att[normed_rows, :] = (ct_rows[r].astype(F32) * modf[2:3, :]).astype(BF)
        return carry

    lax.fori_loop(0, frames, gated_step, 0)

    for cols in col_tiles:
        qkv[:, cols] = dot(att[...], wout[cols, :], NT).astype(BF)
    for h in range(HEADS):
        dop[:, h * LANES : (h + 1) * LANES] = padded(qkv, h * head)

    start(oz_c[1])
    segments = part_send.shape[0]
    per = HEADS // segments

    def back_begin(h):
        do = dop[:, spot_of(h)] * inverse[h]
        total = jnp.sum((do * op[:, spot_of(h)]).T, axis=0, keepdims=True)
        do = do.astype(BF)
        return do, total, dot(head_keys(vp, h), do, NT)

    def back_end(h, seg, j, do, total, dp):
        spot = spot_of(h)
        p = probs[h]
        ds = (p * (dp - total)).astype(BF)
        dv = dot(p, do, NN)
        dk = dot(ds, qp[:, spot], NN) * factor
        op[:, spot] = (dot(head_keys(kp, h), ds, TN) * factor).T.astype(BF)
        dk_own[:, spot] = dk[:half]
        dv_own[:, spot] = dv[:half]
        part_send[seg, 0, :, spot_of(j)] = dk[half:].astype(BF)
        part_send[seg, 1, :, spot_of(j)] = dv[half:].astype(BF)

    part_c = []
    for seg in range(segments):
        begun = back_begin(seg * per)
        for j in range(per):
            h = seg * per + j
            upcoming = back_begin(h + 1) if j + 1 < per else None
            back_end(h, seg, j, *begun)
            begun = upcoming
        copy = remote(part_send.at[seg], part_recv.at[seg], ps.at[seg], pr.at[seg], other)
        copy.start()
        part_c.append(copy)
    output_on(0)
    for h in range(HEADS):
        qkv[:, h * head : (h + 1) * head] = op[:, h * LANES : h * LANES + head]
    for seg in range(segments):
        part_c[seg].wait_recv()
        for j in range(per):
            h = seg * per + j
            spot = slice(h * LANES, (h + 1) * LANES)
            there = slice(j * LANES, (j + 1) * LANES)
            dk = (dk_own[:, spot] + part_recv[seg, 0, :, there].astype(F32)).astype(BF)
            dv = (dv_own[:, spot] + part_recv[seg, 1, :, there].astype(F32)).astype(BF)
            qkv[:, width + h * head : width + (h + 1) * head] = dk[:, :head]
            qkv[:, 2 * width + h * head : 2 * width + (h + 1) * head] = dv[:, :head]

    for cols in col_tiles:
        att[:, cols] = dot(qkv[:, : 3 * width], wqkv[cols, :], NT).astype(BF)


    gz_c = from_frames(grad_stage, grad_ref, gs, gr, 0, whole)
    for r in range(zs):
        _, xhat, inv = norm_parts(r)
        dhat = att[r * rows : (r + 1) * rows, :].astype(F32) * (1.0 + modf[1:2, :])
        m1 = jnp.mean(dhat, axis=-1, keepdims=True)
        m2 = jnp.mean(dhat * xhat, axis=-1, keepdims=True)
        grad_stage[r] = (ct_rows[r].astype(F32) + inv * (dhat - m1 - xhat * m2)).astype(BF)
        gz_c[r].start()

    for i in range(2):
        if i == 1:
            output_on(1)
        wait_recv(o1_c[i])
        pass_on(o1_recv[i], starts[4], o2_send[i])
        start(o2_c[i])
    for i, cols in enumerate(parts):
        wait_recv(o2_c[i])
        join_frames(o2_recv[i], starts[5], out_ref, cols)
    wait_recv(gz_c)

    for copies in [x_c, mod_c, gz_c] + c1_c + c2_c + cz_c + oz_c + o1_c + o2_c:
        wait_send(copies)
    k_c.wait_send()
    v_c.wait_send()
    for copy in part_c:
        copy.wait_send()


def place(out_from, grad_from, out_ref, grad_ref, held, in_sem, out_sem):
    arrays = [(out_from, out_ref), (grad_from, grad_ref)]
    spots = [(n, i) for i in range(out_ref.shape[0]) for n in range(2)]
    come = [pltpu.make_async_copy(arrays[n][0].at[i], held.at[n, i], in_sem.at[n, i]) for n, i in spots]
    go = [pltpu.make_async_copy(held.at[n, i], arrays[n][1].at[i], out_sem.at[n, i]) for n, i in spots]
    for copy in come:
        copy.start()
    for before, after in zip(come, go):
        before.wait()
        after.start()
    for copy in go:
        copy.wait()


def local(latents, route, counts, modulation, w_qkv, w_out, cotangent):
    frames, rows, width = latents.shape
    groups = lax.axis_size("grp")
    half = frames * rows
    padded = HEADS * LANES
    segments = 2
    piece = (frames, rows, width)
    middle = -(-width // LANES // 2) * LANES
    widths = (middle, width - middle)
    dma = pltpu.SemaphoreType.DMA
    vmem = pltpu.VMEM
    block = jax.ShapeDtypeStruct(piece, BF)
    scratch = [vmem(w_qkv.shape, BF), vmem(w_out.shape, BF), vmem(piece, BF)]
    scratch += [tuple(vmem((groups, rows // 2, some), BF) for some in widths)] * 8
    scratch += [vmem(piece, BF)] * 3 + [tuple(vmem((frames, rows, some), BF) for some in widths), vmem(piece, BF)]
    scratch += [vmem((groups, 3, width), F32)] * 2
    scratch += [
        vmem((8, width), F32),
        vmem(piece, BF),
        vmem((half, width), BF),
        vmem((half, 3 * width + LANES), BF),
        vmem((half, padded), BF),
        vmem((2, half, padded), BF),
        vmem((2, half, padded), BF),
        vmem((HEADS, 2 * half, half), BF),
        vmem((half, padded), BF),
        vmem((half, width), BF),
        vmem((half, padded), BF),
        vmem((HEADS, half, LANES), F32),
        vmem((half, padded), F32),
        vmem((half, padded), F32),
        vmem((segments, 2, half, padded // segments), BF),
        vmem((segments, 2, half, padded // segments), BF),
        vmem((1, LANES), jnp.int32),
        pltpu.SMEM((1, LANES), jnp.int32),
        dma((4,)),
    ]
    along_z, across = dma((2, frames)), dma((2, groups))
    scratch += [along_z] * 2 + [dma((groups,))] * 2 + [across] * 4 + [along_z] * 2 + [dma((2,))] * 2
    scratch += [along_z] * 2 + [across] * 4 + [dma((segments,))] * 2 + [along_z] * 2
    in_vmem = pl.BlockSpec(memory_space=vmem)
    in_smem = pl.BlockSpec(memory_space=pltpu.SMEM)
    anywhere = pl.BlockSpec(memory_space=pl.ANY)
    results = pl.pallas_call(
        functools.partial(kernel, groups),
        out_shape=(block, block),
        in_specs=[in_smem, in_smem, in_vmem, anywhere, anywhere, in_vmem, anywhere, anywhere],
        out_specs=(in_vmem, in_vmem),
        scratch_shapes=scratch,
        compiler_params=pltpu.CompilerParams(
            collective_id=0, has_side_effects=True, vmem_limit_bytes=60 * 1024 * 1024
        ),
    )(route, counts, route.reshape(1, -1), latents, cotangent, modulation.transpose(1, 0, 2), w_qkv, w_out)
    return pl.pallas_call(
        place,
        out_shape=(block, block),
        in_specs=[anywhere, anywhere],
        out_specs=(anywhere, anywhere),
        scratch_shapes=[vmem((2,) + piece, BF), dma((2, frames)), dma((2, frames))],
        compiler_params=pltpu.CompilerParams(vmem_limit_bytes=60 * 1024 * 1024),
    )(*results)


def solution(mesh):
    rows = P("grp", "sp", None)
    return jax.shard_map(
        local,
        mesh=mesh,
        in_specs=(rows, P(), P("grp", None), P("grp", None, None), P(), P(), rows),
        out_specs=(rows, rows),
        check_vma=False,
    )
```
